512 devices in a mesh: expert: 16 (over x, y), fsdp: 32 (over z, core).
Axes of the slice: x: 4, y: 4, z: 16, core: 2. Of those that a mesh axis runs over, the one named last changes fastest.
Arguments:
- tokens: bfloat16 [4096, 4096], P('fsdp', 'expert'), may hold values from -6 to 6
- segment_ids: int32 [4096], replicated, may hold values from 0 to 3, never falling along the last dimension, each value on 1 to 2048 neighbouring positions
- w_in_x: bfloat16 [4096, 8192], P('fsdp', 'expert'), may hold values from -0.09375 to 0.09375
- w_in_z: bfloat16 [4096, 8192], P('fsdp', 'expert'), may hold values from -0.09375 to 0.09375
- conv_weight: float32 [4, 8192], P(None, 'expert'), may hold values from -3 to 3
- conv_bias: float32 [8192], P('expert'), may hold values from -3 to 3
- w_xproj: bfloat16 [8192, 288], P('expert'), may hold values from -0.0625 to 0.0625
- w_dt: bfloat16 [256, 8192], P(None, 'expert'), may hold values from -0.375 to 0.375
- dt_bias: float32 [8192], P('expert'), may hold values from -4 to 1
- a_rate: float32 [8192, 16], P('expert'), may hold values from 0.002 to 2
- d_skip: float32 [8192], P('expert'), may hold values from 0.5 to 1.5
- w_out: bfloat16 [8192, 4096], P('expert', 'fsdp'), may hold values from -0.0625 to 0.0625
Outputs:
- mixed: bfloat16 [4096, 4096], P('fsdp', 'expert')
The draws below stay inside these ranges and needn't reach their ends.
Inputs may be any that keep to these rules, and one draw needn't show every extreme that they name: `segment_ids`: document ids never fall along the sequence; each document has at most 2048 tokens, and one has exactly that many.
All inputs are finite; a program needn't handle non-finite values.
Results may differ from the reference program's by a relative error of at most 0.03.
Values may be sent and summed in bfloat16 or wider, within the bound.
A program may use at most 64 MiB of HBM per device.

```python
import math
import jax
import jax.numpy as jnp
import numpy as np
from jax import lax

D = 4096
INNER = 8192
STATE = 16
RANK = 256
KERNEL = 4
TOKENS = 4096
N_EXPERT = 16


def level_of(key, shape, split, smallest, largest):
    def one(position, parts):
        heights = jax.random.uniform(jax.random.fold_in(jax.random.fold_in(key, 6), position), (parts,), jnp.float32, smallest / len(split), largest / len(split))
        return jnp.repeat(jnp.exp(heights), shape[position] // parts).reshape((-1,) + (1,) * (len(shape) - position - 1))

    level = one(*split[0])
    for cut in split[1:]:
        level = level * one(*cut)
    return level


def profile(count, total, reach, lean):
    portions = [(1 << 20) // math.isqrt(rank ** lean) + 1 for rank in range(2, count + 1)]
    rest, given = total - reach - (count - 1), [1] * (count - 1)
    while rest > 0:
        free = [i for i in range(count - 1) if given[i] < reach]
        whole, budget = sum([portions[i] for i in free]), rest
        for i in free:
            more = min(reach - given[i], max(1, budget * portions[i] // whole), rest)
            given[i] = given[i] + more
            rest = rest - more
    return np.array([reach] + given)


def ragged(key, count, total, most, slope):
    if count == 2:
        one = jax.random.randint(key, (), max(1, total - most), min(most, total - 1) + 1)
        return jnp.stack([one, total - one])
    lengths = jnp.asarray(profile(count, total, most, slope), jnp.int32)
    pairs = (count - 1) // 2
    source_of, receiver = lengths[1:1 + 2 * pairs:2], lengths[2:2 + 2 * pairs:2]
    slack = jnp.minimum(source_of - 1, most - receiver)
    passed = jax.random.randint(jax.random.fold_in(key, 1), (pairs,), 0, 1 << 20) % (slack + 1)
    lengths = lengths.at[1:1 + 2 * pairs:2].set(source_of - passed).at[2:2 + 2 * pairs:2].set(receiver + passed)
    return lengths[jax.random.permutation(jax.random.fold_in(key, 2), count)]


def normal_values(rng, shape, deviation, reach, shards=(), dtype=jnp.bfloat16):
    drawn = jax.random.normal(rng, shape, jnp.float32) * deviation
    if len(shards) > 0:
        drawn = level_of(rng, shape, shards, -0.22, 0.18) * drawn
    return jnp.clip(drawn, min=-reach, max=reach).astype(dtype)


def setup_inputs(seed: int = 0) -> dict:
    key_of = jax.random.split(jax.random.key(seed), 13)
    tokens = normal_values(key_of[0], (TOKENS, D), 1.0, 6.0, ((0, 32), (1, 16)))
    segment_ids = jnp.searchsorted(jnp.cumsum(ragged(key_of[1], 4, TOKENS, TOKENS // 2, 2)), jnp.arange(TOKENS), side="right").astype(jnp.int32)
    w_in_x = normal_values(key_of[2], (D, INNER), D ** -0.5, 0.09375, ((0, 32), (1, 16)))
    w_in_z = normal_values(key_of[3], (D, INNER), D ** -0.5, 0.09375, ((0, 32), (1, 16)))
    conv_weight = normal_values(key_of[4], (KERNEL, INNER), 0.5, 3.0, ((1, 16),), jnp.float32)
    conv_bias = normal_values(key_of[5], (INNER,), 0.5, 3.0, ((0, 16),), jnp.float32)
    w_xproj = normal_values(key_of[6], (INNER, RANK + 2 * STATE), INNER ** -0.5, 0.0625, ((0, 16),))
    w_dt = normal_values(key_of[7], (RANK, INNER), RANK ** -0.5, 0.375, ((1, 16),))
    dt_bias = jnp.clip(-4.0 + 5.0 * jax.random.uniform(key_of[8], (INNER,), jnp.float32) ** level_of(key_of[8], (INNER,), ((0, 16),), -0.2, 0.2), -4.0, 1.0)
    a_rate = jnp.clip(jnp.exp(math.log(2.0) - 6.9077552 * jax.random.uniform(key_of[9], (INNER, STATE), jnp.float32) ** level_of(key_of[9], (INNER, STATE), ((0, 16),), -0.2, 0.2)), 0.002, 2.0)
    d_skip = jnp.clip(0.5 + 1.0 * jax.random.uniform(key_of[10], (INNER,), jnp.float32) ** level_of(key_of[10], (INNER,), ((0, 16),), -0.2, 0.2), 0.5, 1.5)
    w_out = normal_values(key_of[11], (INNER, D), INNER ** -0.5, 0.0625, ((0, 16), (1, 32)))
    return {"tokens": tokens, "segment_ids": segment_ids, "w_in_x": w_in_x, "w_in_z": w_in_z, "conv_weight": conv_weight, "conv_bias": conv_bias, "w_xproj": w_xproj, "w_dt": w_dt, "dt_bias": dt_bias, "a_rate": a_rate, "d_skip": d_skip, "w_out": w_out}


def reference(tokens, segment_ids, w_in_x, w_in_z, conv_weight, conv_bias, w_xproj, w_dt, dt_bias, a_rate, d_skip, w_out):
    x_in = jnp.dot(tokens, w_in_x, preferred_element_type=jnp.float32).astype(jnp.bfloat16)
    z_in = jnp.dot(tokens, w_in_z, preferred_element_type=jnp.float32).astype(jnp.bfloat16)
    padded = jnp.concatenate([jnp.zeros((KERNEL - 1, INNER), jnp.bfloat16), x_in], 0).astype(jnp.float32)
    padded_ids = jnp.concatenate([jnp.full((KERNEL - 1,), -1, jnp.int32), segment_ids.astype(jnp.int32)], 0)
    conv_out = jnp.zeros((TOKENS, INNER), jnp.float32) + conv_bias[None, :]
    for offset in range(KERNEL):
        same_doc = (padded_ids[offset:offset + TOKENS] == segment_ids).astype(jnp.float32)
        conv_out = conv_out + conv_weight[offset][None, :] * padded[offset:offset + TOKENS] * same_doc[:, None]
    x_act = jax.nn.silu(conv_out).astype(jnp.bfloat16)
    projected = jnp.dot(x_act, w_xproj, preferred_element_type=jnp.float32)
    dt_low = projected[:, :RANK].astype(jnp.bfloat16)
    b_in = projected[:, RANK:RANK + STATE]
    c_out = projected[:, RANK + STATE:]
    delta = jax.nn.softplus(jnp.dot(dt_low, w_dt, preferred_element_type=jnp.float32) + dt_bias[None, :])
    keep_mask = (padded_ids[KERNEL - 1:] == padded_ids[KERNEL - 2:-1]).astype(jnp.float32)
    x_float = x_act.astype(jnp.float32)

    def scan_step(carried, inputs):
        delta_t, x_t, b_t, c_t, keep_t = inputs
        decay = jnp.exp(-delta_t[:, None] * a_rate) * keep_t
        carried = decay * carried + (delta_t * x_t)[:, None] * b_t[None, :]
        return carried, jnp.sum(carried * c_t[None, :], axis=1)

    start_state = jnp.zeros((INNER, STATE), jnp.float32)
    _, outputs = lax.scan(scan_step, start_state, (delta, x_float, b_in, c_out, keep_mask))
    scanned = outputs + d_skip[None, :] * x_float
    gated = (scanned * jax.nn.silu(z_in.astype(jnp.float32))).astype(jnp.bfloat16)
    block_size = INNER // N_EXPERT

    def add_block(index, running):
        first_row = (index * block_size).astype(jnp.int32)
        gated_block = lax.dynamic_slice_in_dim(gated, first_row, block_size, 1)
        weight_block = lax.dynamic_slice_in_dim(w_out, first_row, block_size, 0)
        partial_sum = jnp.dot(gated_block, weight_block, preferred_element_type=jnp.float32).astype(jnp.bfloat16)
        partial_sum = lax.optimization_barrier(partial_sum)
        return running + partial_sum.astype(jnp.float32)

    mixed = lax.fori_loop(0, N_EXPERT, add_block, jnp.zeros((TOKENS, D), jnp.float32))
    return mixed.astype(jnp.bfloat16)
```

```python
import functools
import math

import jax
import jax.numpy as jnp
from jax import lax
from jax.experimental import pallas as pl
from jax.experimental.pallas import tpu as pltpu
from jax.sharding import PartitionSpec as P

F32 = jnp.float32
BF16 = jnp.bfloat16
FAR = 1e30
LOG2E = 1.0 / math.log(2.0)
MESH = pl.DeviceIdType.MESH


def silu(v):
    return v * jax.nn.sigmoid(v)


def dot(a, b):
    return jnp.dot(a, b, preferred_element_type=F32)


def kernel(
    sizes,
    tok, wx, wz, wo, conv_w, conv_b, wxp, wdt, dt_bias, rates, d_skip, masks,
    out,
    TOK, WX, WZ, WO, AX, AZ, XP, HALO, ZS, XA, PP, PA, PS, RB, PR,
    DD, DX, SC, Y, HE, PE, KM, KR, G, XS, XR, MO, OS, RO,
    local_sem, pair_s, pair_r, tok_s, tok_r, fwd_s, fwd_r, ring_s, ring_r,
    halo_s, halo_r, half_s, half_r, sum_s, sum_r, all_s, all_r,
    state_s, state_r, swap_s, swap_r, out_s, out_r,
):
    NE, NZ, TL, KR_, CH, OC, R, N = sizes
    T, J, H = 2 * TL, TL // 4, NZ // 2
    PW = R + 128
    hops = [1, 1]
    while sum(hops) < H:
        hops.append(2 * hops[-1])
    e = lax.axis_index("expert")
    f = lax.axis_index("fsdp")
    z = lax.div(f, 2)
    c = lax.rem(f, 2)
    o = 1 - c

    def zmod(v):
        return lax.rem(v + 2 * NZ, NZ)

    def emod(v):
        return lax.rem(v + 2 * NE, NE)

    def at(e_, z_, c_):
        return (e_, 2 * z_ + c_)

    def remote(src, dst, ss, rs, dev):
        return pltpu.make_async_remote_copy(
            src_ref=src, dst_ref=dst, send_sem=ss, recv_sem=rs, device_id=dev, device_id_type=MESH
        )

    def span(i, n, unit=None):
        return pl.ds(pl.multiple_of(i * n, n), n)

    partner = at(e, z, o)
    me = at(e, z, c)

    own = [
        pltpu.make_async_copy(wx.at[:, span(c, CH)], WX.at[z, span(c, KR_)], local_sem.at[0]),
        pltpu.make_async_copy(wz.at[:, span(c, CH)], WZ.at[z, span(c, KR_)], local_sem.at[1]),
        pltpu.make_async_copy(wo.at[span(c, CH)], WO.at[z, :, span(c, OC)], local_sem.at[2]),
        pltpu.make_async_copy(tok, TOK.at[e, span(c, TL)], local_sem.at[3]),
    ]
    for copy in own:
        copy.start()

    barrier = pltpu.get_barrier_semaphore()
    friends = [partner]
    for d in sorted(set(hops)):
        friends += [at(e, zmod(z + d), c), at(e, zmod(z - d), c)]
    for dev in friends:
        pl.semaphore_signal(barrier, inc=1, device_id=dev, device_id_type=MESH)

    def greet(k, _):
        pl.semaphore_signal(
            barrier, inc=1, device_id=at(emod(e + k), z, c), device_id_type=MESH
        )
        return 0

    lax.fori_loop(1, NE, greet, 0)
    pl.semaphore_wait(barrier, len(friends) + NE - 1)

    pairs = [
        remote(wx.at[:, span(o, CH)], WX.at[z, span(c, KR_)], pair_s.at[0], pair_r.at[0], partner),
        remote(wz.at[:, span(o, CH)], WZ.at[z, span(c, KR_)], pair_s.at[1], pair_r.at[1], partner),
        remote(wo.at[span(o, CH)], WO.at[z, :, span(c, OC)], pair_s.at[2], pair_r.at[2], partner),
    ]
    pairs_in = [
        remote(wx.at[:, span(o, CH)], WX.at[z, span(o, KR_)], pair_s.at[0], pair_r.at[0], partner),
        remote(wz.at[:, span(o, CH)], WZ.at[z, span(o, KR_)], pair_s.at[1], pair_r.at[1], partner),
        remote(wo.at[span(o, CH)], WO.at[z, :, span(o, OC)], pair_s.at[2], pair_r.at[2], partner),
    ]
    for copy in pairs:
        copy.start()

    def tok_send(k):
        return remote(
            tok, TOK.at[e, span(c, TL)], tok_s.at[k], tok_r.at[k], at(emod(e + k), z, c)
        )

    def tok_in(k):
        return remote(
            tok, TOK.at[emod(e - k), span(c, TL)], tok_s.at[k], tok_r.at[k], partner
        )

    def tok_fwd(k):
        b = emod(e - k)
        return remote(
            TOK.at[b, span(c, TL)], TOK.at[b, span(c, TL)], fwd_s.at[k], fwd_r.at[k], partner
        )

    def tok_fwd_in(k):
        b = emod(e - k)
        return remote(
            TOK.at[b, span(o, TL)], TOK.at[b, span(o, TL)], fwd_s.at[k], fwd_r.at[k], partner
        )

    def each(lo, hi, fn):
        def body(k, _):
            fn(k)
            return 0

        lax.fori_loop(lo, hi, body, 0)

    each(1, NE, lambda k: tok_send(k).start())

    stacks = [WX, WZ, WO]

    def hop(p, d, s):
        sign = 1 - 2 * d
        block = zmod(z - sign * (s - 1))
        return remote(
            stacks[p].at[block], stacks[p].at[block],
            ring_s.at[p, d, s], ring_r.at[p, d, s], at(e, zmod(z + sign), c),
        )

    def arrive(p, d, s):
        sign = 1 - 2 * d
        block = zmod(z - sign * s)
        remote(
            stacks[p].at[block], stacks[p].at[block],
            ring_s.at[p, d, s], ring_r.at[p, d, s], at(e, zmod(z + sign), c),
        ).wait_recv()

    def add(block, first=False):
        t = TOK[block]
        if first:
            AX[...] = dot(t, WX[block])
            AZ[...] = dot(t, WZ[block])
        else:
            AX[...] += dot(t, WX[block])
            AZ[...] += dot(t, WZ[block])

    for p in (0, 1):
        own[p].wait()
        pairs_in[p].wait_recv()
        hop(p, 0, 1).start()
        hop(p, 1, 1).start()
    own[3].wait()
    tok_fwd(0).start()

    done = 0
    for s in range(1, H):
        for p in (0, 1):
            for d in (0, 1):
                arrive(p, d, s)
                if s < H - 1 or p == d:
                    hop(p, d, s + 1).start()
        if s == H - 1:
            own[2].wait()
            pairs_in[2].wait_recv()
            hop(2, 0, 1).start()
            hop(2, 1, 1).start()
        if s == 1:

            def relay(k):
                tok_in(k).wait_recv()
                tok_fwd(k).start()

            each(1, NE, relay)
        if s == min(2, H - 1):
            each(0, NE, lambda k: tok_fwd_in(k).wait_recv())
            add(z, first=True)
        if s > 2:
            add(zmod(z - (s - 2)))
            add(zmod(z + (s - 2)))
            done = s - 2
    for s in range(done + 1, H):
        add(zmod(z - s))
        add(zmod(z + s))
    arrive(0, 0, H)
    arrive(1, 1, H)
    add(zmod(z + H))

    def pump(s):
        if s < H:
            arrive(2, 0, s)
            hop(2, 0, s + 1).start()
            arrive(2, 1, s)
            if s < H - 1:
                hop(2, 1, s + 1).start()
        elif s == H:
            arrive(2, 0, s)

    row = lax.broadcasted_iota(jnp.int32, (T, T), 0)
    col = lax.broadcasted_iota(jnp.int32, (T, T), 1)
    perm = (col == lax.rem(row, 8) * J + lax.div(row, 8)).astype(F32).astype(BF16)
    XP[...] = dot(perm, AX[...].astype(BF16))
    rim = XP.at[pl.ds((J - 3) * 8, 24)]
    halo = remote(rim, HALO, halo_s, halo_r, at(e, zmod(z + 1), c))
    halo.start()
    ZS[...] = silu(dot(perm, AZ[...].astype(BF16)))
    pump(1)
    halo.wait_recv()
    lane_c = span(c, CH)
    top = lax.broadcasted_iota(jnp.int32, (8, CH), 0) == 0
    early = []
    for i in range(3):
        mine = pltpu.roll(XP[(J - 3 + i) * 8 : (J - 2 + i) * 8], 1, 0)
        theirs = pltpu.roll(HALO[i * 8 : (i + 1) * 8], 1, 0)
        early.append(jnp.where(top, theirs, mine))
    ext = jnp.concatenate(early + [XP[...]], 0)
    conv = conv_b[:, lane_c] + conv_w[3:4, lane_c] * ext[24:]
    for k in range(1, 4):
        conv += conv_w[3 - k : 4 - k, lane_c] * ext[24 - 8 * k : 24 - 8 * k + T] * masks[:, k - 1 : k]
    x_act = silu(conv).astype(BF16)
    XA[...] = x_act.astype(F32)
    PP[...] = dot(x_act, wxp[span(c, CH), :])

    half = remote(PP.at[span(o, TL)], PA, half_s.at[0], half_r.at[0], partner)
    half.start()
    pump(2)
    half.wait_recv()
    PS[...] = PP[span(c, TL), :] + PA[...]

    def sum_send(k):
        return remote(
            PS.at[span(emod(e + k), 8)], RB.at[k], sum_s.at[k], sum_r.at[k], at(emod(e + k), z, c)
        )

    each(1, NE, lambda k: sum_send(k).start())
    pump(3)
    each(1, NE, lambda k: sum_send(k).wait_recv())
    total = PS[span(e, 8), :]
    for k in range(1, NE):
        total += RB[k]
    eighth = pl.ds(pl.multiple_of(c * TL + e * 8, 8), 8)
    PR[eighth, :] = total

    def all_send(k):
        return remote(
            PR.at[eighth], PR.at[eighth], all_s.at[k], all_r.at[k], at(emod(e + k), z, c)
        )

    def all_in(k):
        theirs = pl.ds(pl.multiple_of(c * TL + emod(e - k) * 8, 8), 8)
        return remote(PR.at[theirs], PR.at[theirs], all_s.at[k], all_r.at[k], partner)

    each(1, NE, lambda k: all_send(k).start())
    pump(4)
    each(1, NE, lambda k: all_in(k).wait_recv())
    rest = remote(PR.at[span(c, TL)], PR.at[span(c, TL)], half_s.at[1], half_r.at[1], partner)
    rest_in = remote(PR.at[span(o, TL)], PR.at[span(o, TL)], half_s.at[1], half_r.at[1], partner)
    rest.start()
    pump(5)
    rest_in.wait_recv()

    delta = dot(PR[:, :R].astype(BF16), wdt[:, lane_c]) + dt_bias[:, lane_c]
    delta = jnp.maximum(delta, 0.0) + jnp.log1p(jnp.exp(-jnp.abs(delta)))
    DX[...] = delta * XA[...]
    DD[...] = delta + (1.0 - masks[:, 0:1]) * FAR

    slope = [rates[n : n + 1, lane_c] * (-LOG2E) for n in range(N)]

    def forward(j, carry):
        hs, reach = carry
        r = pl.ds(pl.multiple_of(j * 8, 8), 8)
        dd, dx, bc = DD[r, :], DX[r, :], PR[r, R : R + 128]
        reach = reach + dd
        SC[r, :] = reach
        y = jnp.zeros((8, CH), F32)
        later = []
        for n in range(N):
            h = jnp.exp2(dd * slope[n]) * hs[n] + dx * bc[:, n : n + 1]
            y = y + h * bc[:, N + n : N + n + 1]
            later.append(h)
        Y[r, :] = y
        return later, reach

    zero = jnp.zeros((8, CH), F32)
    ends, reach = lax.fori_loop(0, J, forward, ([zero] * N, zero))
    sub = lax.broadcasted_iota(jnp.int32, (8, CH), 0)
    for n in range(N):
        h, p = ends[n], jnp.exp2(reach * slope[n])
        for d in (1, 2, 4):
            before = sub >= d
            h = h + p * jnp.where(before, pltpu.roll(h, d, 0), 0.0)
            p = p * jnp.where(before, pltpu.roll(p, d, 0), 1.0)
        KM[0, n : n + 1, :] = h[7:8]
        HE[n] = jnp.where(top, 0.0, pltpu.roll(h, 1, 0))
        PE[n] = jnp.where(top, 1.0, pltpu.roll(p, 1, 0))
    KM[0, N : N + 8, :] = jnp.broadcast_to(jnp.sum(reach, axis=0, keepdims=True), (8, CH))

    steep = rates[:, lane_c] * (-LOG2E)

    def state_send(i):
        return remote(
            KM.at[i], KR.at[i], state_s.at[i], state_r.at[i], at(e, zmod(z + hops[i]), c)
        )

    for i in range(len(hops)):
        state_send(i).start()
        pump(6 + i)
        state_send(i).wait_recv()
        if i == 0:
            KM[1] = KR[0]
        else:
            decay = jnp.exp2(KM[i, N : N + 1, :] * steep)
            entering = decay * KR[i, :N, :] + KM[i, :N, :]
            KM[i + 1, :N, :] = entering
            KM[i + 1, N : N + 8, :] = KM[i, N : N + 8, :] + KR[i, N : N + 8, :]
    for s in range(6 + len(hops), H + 1):
        pump(s)
    last = len(hops)
    for n in range(N):
        HE[n] = HE[n] + PE[n] * KM[last, n : n + 1, :]

    def correct(j, _):
        r = pl.ds(pl.multiple_of(j * 8, 8), 8)
        reach, bc = SC[r, :], PR[r, R : R + 128]
        y = Y[r, :]
        for n in range(N):
            y = y + jnp.exp2(reach * slope[n]) * HE[n] * bc[:, N + n : N + n + 1]
        Y[r, :] = (y + d_skip[:, lane_c] * XA[r, :]) * ZS[r, :]
        return 0

    lax.fori_loop(0, J, correct, 0)
    back = (col == lax.rem(row, J) * 8 + lax.div(row, J)).astype(F32).astype(BF16)
    G[...] = dot(back, Y[...].astype(BF16)).astype(BF16)

    def swap(k):
        return remote(XS.at[k], XR.at[k], swap_s.at[k], swap_r.at[k], partner)

    def multiply(k):
        w = WO[emod(e + k)]
        XS[k] = dot(G[span(o, TL), :], w).astype(BF16)
        swap(k).start()
        MO[k] = dot(G[span(c, TL), :], w)

    each(0, NE, multiply)

    def out_send(k):
        return remote(OS.at[k], RO.at[k], out_s.at[k], out_r.at[k], at(emod(e + k), z, c))

    def reduce(k):
        swap(k).wait_recv()
        OS[k] = (MO[k] + XR[k].astype(F32)).astype(BF16)

    def reduce_send(k):
        reduce(k)
        out_send(k).start()

    each(1, NE, reduce_send)
    reduce(0)
    result = OS[0].astype(F32)
    for k in range(1, NE):
        out_send(k).wait_recv()
        result += RO[k].astype(F32)
    out[...] = result.astype(BF16)

    for copy in pairs:
        copy.wait_send()
    halo.wait_send()
    half.wait_send()
    rest.wait_send()
    for i in range(len(hops)):
        state_send(i).wait_send()

    def drain(k):
        tok_send(k).wait_send()
        sum_send(k).wait_send()
        all_send(k).wait_send()
        out_send(k).wait_send()

    each(1, NE, drain)

    def drain_pair(k):
        tok_fwd(k).wait_send()
        swap(k).wait_send()

    each(0, NE, drain_pair)

    def drain_ring(s):
        for p in range(3):
            for d in range(2):
                hop(p, d, s).wait_send()

    each(1, H, drain_ring)
    hop(0, 0, H).wait_send()
    hop(1, 1, H).wait_send()
    hop(2, 0, H).wait_send()


def local(
    tokens, segment_ids, w_in_x, w_in_z, conv_weight, conv_bias, w_xproj, w_dt, dt_bias,
    a_rate, d_skip, w_out,
):
    NE, NZ = lax.axis_size("expert"), lax.axis_size("fsdp") // 2
    TL, DC = tokens.shape
    KR_, C2 = w_in_x.shape
    CH, OC, R, N = C2 // 2, w_out.shape[1], w_dt.shape[0], a_rate.shape[1]
    T, J, H = 2 * TL, TL // 4, NZ // 2
    PW = R + 128
    z = lax.axis_index("fsdp") // 2
    padded = jnp.concatenate([jnp.full((3,), -1, jnp.int32), segment_ids], 0)
    window = lax.dynamic_slice_in_dim(padded, z * T, T + 3)
    same = jnp.stack([window[3 - k : 3 - k + T] == window[3:] for k in (1, 2, 3)])
    masks = same.reshape(3, 8, J).transpose(2, 1, 0).reshape(T, 3).astype(F32)
    masks = jnp.pad(masks, ((0, 0), (0, 125)))
    wxp = jnp.pad(w_xproj, ((0, 0), (0, PW - w_xproj.shape[1])))
    rounds = 2 + max(0, H.bit_length() - 2)
    sizes = (NE, NZ, TL, KR_, CH, OC, R, N)
    V = pltpu.VMEM
    dma = pltpu.SemaphoreType.DMA
    any_space = pl.BlockSpec(memory_space=pl.ANY)
    vmem = pl.BlockSpec(memory_space=pltpu.VMEM)
    return pl.pallas_call(
        functools.partial(kernel, sizes),
        out_shape=jax.ShapeDtypeStruct((TL, DC), BF16),
        in_specs=[any_space] * 4 + [vmem] * 8,
        out_specs=vmem,
        scratch_shapes=[
            V((NE, T, DC), BF16),
            V((NZ, 2 * KR_, CH), BF16),
            V((NZ, 2 * KR_, CH), BF16),
            V((NZ, CH, 2 * OC), BF16),
            V((T, CH), F32),
            V((T, CH), F32),
            V((T, CH), F32),
            V((24, CH), F32),
            V((T, CH), F32),
            V((T, CH), F32),
            V((T, PW), F32),
            V((TL, PW), F32),
            V((TL, PW), F32),
            V((NE, 8, PW), F32),
            V((T, PW), F32),
            V((T, CH), F32),
            V((T, CH), F32),
            V((T, CH), F32),
            V((T, CH), F32),
            V((N, 8, CH), F32),
            V((N, 8, CH), F32),
            V((rounds + 1, N + 8, CH), F32),
            V((rounds, N + 8, CH), F32),
            V((T, CH), BF16),
            V((NE, TL, DC), BF16),
            V((NE, TL, DC), BF16),
            V((NE, TL, DC), F32),
            V((NE, TL, DC), BF16),
            V((NE, TL, DC), BF16),
            dma((4,)),
            dma((3,)), dma((3,)),
            dma((NE,)), dma((NE,)),
            dma((NE,)), dma((NE,)),
            dma((3, 2, H + 1)), dma((3, 2, H + 1)),
            dma(()), dma(()),
            dma((2,)), dma((2,)),
            dma((NE,)), dma((NE,)),
            dma((NE,)), dma((NE,)),
            dma((rounds,)), dma((rounds,)),
            dma((NE,)), dma((NE,)),
            dma((NE,)), dma((NE,)),
        ],
        compiler_params=pltpu.CompilerParams(
            collective_id=0, has_side_effects=True, vmem_limit_bytes=48 * 1024 * 1024
        ),
    )(
        tokens, w_in_x, w_in_z, w_out, conv_weight, conv_bias[None, :], wxp, w_dt,
        dt_bias[None, :], a_rate.T, d_skip[None, :], masks,
    )


def solution(mesh):
    placed = (
        P("fsdp", "expert"),
        P(),
        P("fsdp", "expert"),
        P("fsdp", "expert"),
        P(None, "expert"),
        P("expert"),
        P("expert", None),
        P(None, "expert"),
        P("expert"),
        P("expert", None),
        P("expert"),
        P("expert", "fsdp"),
    )
    return jax.shard_map(
        local, mesh=mesh, in_specs=placed, out_specs=P("fsdp", "expert"), check_vma=False
    )
```

```python
import functools
import math

import jax
import jax.numpy as jnp
from jax import lax
from jax.experimental import pallas as pl
from jax.experimental.pallas import tpu as pltpu
from jax.sharding import PartitionSpec as P

F32 = jnp.float32
BF16 = jnp.bfloat16
FAR = 1e30
LOG2E = 1.0 / math.log(2.0)
MESH = pl.DeviceIdType.MESH


def silu(v):
    return v * jax.nn.sigmoid(v)


def dot(a, b):
    return jnp.dot(a, b, preferred_element_type=F32)


def kernel(
    sizes,
    tok, wx, wz, wo, conv_w, conv_b, wxp, wdt, dt_bias, rates, d_skip, masks,
    out,
    TOK, WX, WZ, WO, AX, AZ, XP, HALO, XA, PB, RB, GB, PR,
    DD, DX, SC, Y, HE, PE, KM, KR, G, XS, XR, MO, OS, RO,
    local_sem, pair_s, pair_r, tok_s, tok_r, fwd_s, fwd_r, ring_s, ring_r,
    halo_s, halo_r, sum_s, sum_r, all_s, all_r,
    state_s, state_r, swap_s, swap_r, out_s, out_r,
):
    NE, NZ, TL, KR_, CH, OC, R, N = sizes
    T, J, H = 2 * TL, TL // 4, NZ // 2
    L = (R + 128) // 128
    CR = PB.shape[1]
    near = min(H, 4)
    far = [near * i for i in range(1, H // near)]
    e = lax.axis_index("expert")
    f = lax.axis_index("fsdp")
    z = lax.div(f, 2)
    c = lax.rem(f, 2)
    o = 1 - c

    def zmod(v):
        return lax.rem(v + 2 * NZ, NZ)

    def emod(v):
        return lax.rem(v + 2 * NE, NE)

    def at(e_, z_, c_):
        return (e_, 2 * z_ + c_)

    def remote(src, dst, ss, rs, dev):
        return pltpu.make_async_remote_copy(
            src_ref=src, dst_ref=dst, send_sem=ss, recv_sem=rs, device_id=dev, device_id_type=MESH
        )

    def span(i, n):
        return pl.ds(pl.multiple_of(i * n, n), n)

    def each(lo, hi, fn):
        def body(k, _):
            fn(k)
            return 0

        lax.fori_loop(lo, hi, body, 0)

    partner = at(e, z, o)

    own = [
        pltpu.make_async_copy(wx.at[:, span(c, CH)], WX.at[z, span(c, KR_)], local_sem.at[0]),
        pltpu.make_async_copy(wz.at[:, span(c, CH)], WZ.at[z, span(c, KR_)], local_sem.at[1]),
        pltpu.make_async_copy(wo.at[span(c, CH)], WO.at[z, :, span(c, OC)], local_sem.at[2]),
        pltpu.make_async_copy(tok, TOK.at[e, span(c, TL)], local_sem.at[3]),
    ]
    for copy in own:
        copy.start()

    barrier = pltpu.get_barrier_semaphore()

    def greet(dev):
        pl.semaphore_signal(barrier, inc=1, device_id=dev, device_id_type=MESH)

    friends = [partner]
    for d in sorted(set(range(1, near + 1)) | set(far)):
        friends += [at(e, zmod(z + d), c), at(e, zmod(z - d), c)]
    count = 1 + 2 * len(set(range(1, near + 1)) | set(far))
    if near == H and NZ == 2 * H and H < 3:
        friends = friends[:-1]
        count -= 1
    for dev in friends:
        greet(dev)

    def greet_plane(k):
        greet(at(emod(e + k), z, c))
        greet(at(emod(e + k), z, o))

    each(1, NE, greet_plane)
    pl.semaphore_wait(barrier, count + 2 * (NE - 1))

    def pair(p, side):
        src = [wx.at[:, span(o, CH)], wz.at[:, span(o, CH)], wo.at[span(o, CH)]][p]
        dst = [WX.at[z, span(side, KR_)], WZ.at[z, span(side, KR_)], WO.at[z, :, span(side, OC)]][p]
        return remote(src, dst, pair_s.at[p], pair_r.at[p], partner)

    pair(0, c).start()

    stacks = [WX, WZ, WO]

    def piece(p, block, h):
        rows = stacks[p].shape[1] // 2
        return stacks[p].at[block, span(h, rows)]

    def hop(p, d, s, h):
        sign = 1 - 2 * d
        block = zmod(z - sign * (s - 1))
        return remote(
            piece(p, block, h), piece(p, block, h),
            ring_s.at[p, d, s, h], ring_r.at[p, d, s, h], at(e, zmod(z + sign), c),
        )

    def arrive(p, d, s, h):
        sign = 1 - 2 * d
        block = zmod(z - sign * s)
        remote(
            piece(p, block, h), piece(p, block, h),
            ring_s.at[p, d, s, h], ring_r.at[p, d, s, h], at(e, zmod(z + sign), c),
        ).wait_recv()

    own[0].wait()
    hop(0, 0, 1, c).start()
    hop(0, 1, 1, c).start()
    pair(1, c).start()
    pair(2, c).start()

    def tok_send(k):
        return remote(
            tok, TOK.at[e, span(c, TL)], tok_s.at[k], tok_r.at[k], at(emod(e + k), z, c)
        )

    def tok_in(k):
        return remote(
            tok, TOK.at[emod(e - k), span(c, TL)], tok_s.at[k], tok_r.at[k], partner
        )

    def tok_fwd(k):
        b = emod(e - k)
        return remote(
            TOK.at[b, span(c, TL)], TOK.at[b, span(c, TL)], fwd_s.at[k], fwd_r.at[k], partner
        )

    def tok_fwd_in(k):
        b = emod(e - k)
        return remote(
            TOK.at[b, span(o, TL)], TOK.at[b, span(o, TL)], fwd_s.at[k], fwd_r.at[k], partner
        )

    pair(0, o).wait_recv()
    hop(0, 0, 1, o).start()
    hop(0, 1, 1, o).start()
    each(1, NE, lambda k: tok_send(k).start())
    own[3].wait()
    tok_fwd(0).start()

    def begin(p):
        own[p].wait()
        pair(p, o).wait_recv()
        for h in (0, 1):
            for d in (0, 1):
                hop(p, d, 1, h).start()

    def step(p, s):
        for h in (0, 1):
            for d in (0, 1):
                if s < H or d == h:
                    arrive(p, d, s, h)
                    if s < H - 1 or (s == H - 1 and d == h):
                        hop(p, d, s + 1, h).start()

    def add(acc, w, block, first=False):
        product = dot(TOK[block], w[block])
        acc[...] = product if first else acc[...] + product

    def add_step(acc, w, s):
        add(acc, w, zmod(z - s))
        if s < H:
            add(acc, w, zmod(z + s))

    done = 0
    for s in range(1, H + 1):
        step(0, s)
        if s == H - 1:
            begin(1)
        if s == 1:

            def relay(k):
                tok_in(k).wait_recv()
                tok_fwd(k).start()

            each(1, NE, relay)
        if s == min(3, H):
            each(0, NE, lambda k: tok_fwd_in(k).wait_recv())
            add(AX, WX, z, first=True)
        if s > 3:
            for s_ in range(done + 1, s - 1):
                add_step(AX, WX, s_)
            done = max(done, s - 2)
    for s in range(done + 1, H + 1):
        add_step(AX, WX, s)

    events = [(1, s) for s in range(1, H + 1)] + [(2, s) for s in range(1, H + 1)]
    position = [0]

    def pump(upto):
        while position[0] < min(upto, len(events)):
            p, s = events[position[0]]
            position[0] += 1
            step(p, s)
            if p == 1:
                if s == H - 1:
                    begin(2)
                if s == 1:
                    add(AZ, WZ, z, first=True)
                add_step(AZ, WZ, s)

    row = lax.broadcasted_iota(jnp.int32, (T, T), 0)
    col = lax.broadcasted_iota(jnp.int32, (T, T), 1)
    perm = (col == lax.rem(row, 8) * J + lax.div(row, 8)).astype(F32).astype(BF16)
    XP[...] = dot(perm, AX[...].astype(BF16))
    rim = XP.at[pl.ds((J - 3) * 8, 24)]
    halo = remote(rim, HALO, halo_s, halo_r, at(e, zmod(z + 1), c))
    halo.start()
    pump(1)
    halo.wait_recv()
    lane_c = span(c, CH)
    top = lax.broadcasted_iota(jnp.int32, (8, CH), 0) == 0
    early = []
    for i in range(3):
        mine = pltpu.roll(XP[(J - 3 + i) * 8 : (J - 2 + i) * 8], 1, 0)
        theirs = pltpu.roll(HALO[i * 8 : (i + 1) * 8], 1, 0)
        early.append(jnp.where(top, theirs, mine))
    ext = jnp.concatenate(early + [XP[...]], 0)
    conv = conv_b[:, lane_c] + conv_w[3:4, lane_c] * ext[24:]
    for k in range(1, 4):
        conv += conv_w[3 - k : 4 - k, lane_c] * ext[24 - 8 * k : 24 - 8 * k + T] * masks[:, k - 1 : k]
    x_act = silu(conv).astype(BF16)
    XA[...] = x_act.astype(F32)
    PR[...] = dot(x_act, wxp[span(c, CH), :])

    blank = [jnp.zeros((CR - 8 * L, 128), F32)] if CR > 8 * L else []

    def pack(q):
        rows = span(q, 8)
        tiles = [PR[rows, l * 128 : (l + 1) * 128] for l in range(L)]
        PB[q] = jnp.concatenate(tiles + blank, 0).astype(BF16)

    each(0, 2 * NE, pack)

    def plane(k, rel):
        core = c if rel == 0 else o
        return emod(e + k), core

    def sum_send(k, rel):
        e_, core = plane(k, rel)
        return remote(
            PB.at[core * NE + e_], RB.at[rel * NE + k],
            sum_s.at[rel, k], sum_r.at[rel, k], at(e_, z, core),
        )

    mine = c * NE + e

    def all_send(k, rel):
        e_, core = plane(k, rel)
        return remote(
            GB.at[mine], GB.at[mine], all_s.at[rel, k], all_r.at[rel, k], at(e_, z, core)
        )

    def all_in(k, rel):
        e_, core = plane(-k, rel)
        theirs = core * NE + e_
        return remote(
            GB.at[theirs], GB.at[theirs], all_s.at[rel, k], all_r.at[rel, k], at(e_, z, core)
        )

    def everyone(fn):
        fn(0, 1)

        def both(k):
            fn(k, 1)
            fn(k, 0)

        each(1, NE, both)

    everyone(lambda k, rel: sum_send(k, rel).start())
    pump(3)
    everyone(lambda k, rel: sum_send(k, rel).wait_recv())
    total = PB[mine].astype(F32)
    for k in range(1, 2 * NE):
        total += RB[k].astype(F32)
    GB[mine] = total.astype(BF16)
    everyone(lambda k, rel: all_send(k, rel).start())
    pump(4)
    everyone(lambda k, rel: all_in(k, rel).wait_recv())

    def unpack(q):
        chunk = GB[q].astype(F32)
        for l in range(L):
            PR[span(q, 8), l * 128 : (l + 1) * 128] = chunk[8 * l : 8 * l + 8]

    each(0, 2 * NE, unpack)
    pump(5)
    delta = dot(PR[:, :R].astype(BF16), wdt[:, lane_c]) + dt_bias[:, lane_c]
    delta = jnp.maximum(delta, 0.0) + jnp.log1p(jnp.exp(-jnp.abs(delta)))
    DX[...] = delta * XA[...]
    DD[...] = delta + (1.0 - masks[:, 0:1]) * FAR

    slope = [rates[n : n + 1, lane_c] * (-LOG2E) for n in range(N)]

    def forward(j, carry):
        hs, reach = carry
        r = pl.ds(pl.multiple_of(j * 8, 8), 8)
        dd, dx, bc = DD[r, :], DX[r, :], PR[r, R : R + 128]
        reach = reach + dd
        SC[r, :] = reach
        y = jnp.zeros((8, CH), F32)
        later = []
        for n in range(N):
            h = jnp.exp2(dd * slope[n]) * hs[n] + dx * bc[:, n : n + 1]
            y = y + h * bc[:, N + n : N + n + 1]
            later.append(h)
        Y[r, :] = y
        return later, reach

    zero = jnp.zeros((8, CH), F32)
    middle = lax.fori_loop(0, J // 2, forward, ([zero] * N, zero))
    pump(6)
    ends, reach = lax.fori_loop(J // 2, J, forward, middle)
    sub = lax.broadcasted_iota(jnp.int32, (8, CH), 0)
    states = []
    for n in range(N):
        h, p = ends[n], jnp.exp2(reach * slope[n])
        for d in (1, 2, 4):
            before = sub >= d
            h = h + p * jnp.where(before, pltpu.roll(h, d, 0), 0.0)
            p = p * jnp.where(before, pltpu.roll(p, d, 0), 1.0)
        HE[n] = jnp.where(top, 0.0, pltpu.roll(h, 1, 0))
        PE[n] = jnp.where(top, 1.0, pltpu.roll(p, 1, 0))
        states.append(h[7:8])
    span_sum = jnp.broadcast_to(jnp.sum(reach, axis=0, keepdims=True), (N, CH))
    KM[0] = jnp.concatenate(states + [span_sum], 0).astype(BF16)

    steep = rates[:, lane_c] * (-LOG2E)

    def state_send(i):
        d = i + 1 if i < near else far[i - near]
        return remote(
            KM.at[0 if i < near else 1], KR.at[i], state_s.at[i], state_r.at[i],
            at(e, zmod(z + d), c),
        )

    def join(earlier, latter):
        both = latter.astype(F32)
        h, reach = both[:N], both[N:]
        if earlier is None:
            return h, reach
        return jnp.exp2(reach * steep) * earlier[0] + h, earlier[1] + reach

    for i in range(near):
        state_send(i).start()
    pump(8)
    for i in range(near):
        state_send(i).wait_recv()
    entering = None
    for i in range(near - 1, -1, -1):
        entering = join(entering, KR[i])
    if far:
        KM[1] = jnp.concatenate(entering, 0).astype(BF16)
        for i in range(near, near + len(far)):
            state_send(i).start()
        pump(9)
        for i in range(near, near + len(far)):
            state_send(i).wait_recv()
        combined = None
        for i in range(near + len(far) - 1, near - 1, -1):
            combined = join(combined, KR[i])
        entering = join(combined, KM[1])
    pump(10)
    for n in range(N):
        HE[n] = HE[n] + PE[n] * entering[0][n : n + 1, :]

    AZ[...] = silu(dot(perm, AZ[...].astype(BF16)))

    def correct(j, _):
        r = pl.ds(pl.multiple_of(j * 8, 8), 8)
        reach, bc = SC[r, :], PR[r, R : R + 128]
        y = Y[r, :]
        for n in range(N):
            y = y + jnp.exp2(reach * slope[n]) * HE[n] * bc[:, N + n : N + n + 1]
        Y[r, :] = (y + d_skip[:, lane_c] * XA[r, :]) * AZ[r, :]
        return 0

    lax.fori_loop(0, J, correct, 0)
    back = (col == lax.rem(row, J) * 8 + lax.div(row, J)).astype(F32).astype(BF16)
    G[...] = dot(back, Y[...].astype(BF16)).astype(BF16)

    def swap(k):
        return remote(XS.at[k], XR.at[k], swap_s.at[k], swap_r.at[k], partner)

    def out_send(k):
        return remote(OS.at[k], RO.at[k], out_s.at[k], out_r.at[k], at(emod(e + k), z, c))

    def group(low, high):
        total = 2 * (high - low + 1) - (low == 0) - (high == H)

        def offset(i):
            i = lax.rem(i + e, total)
            if low == 0:
                return lax.div(i + 1, 2) * (1 - 2 * lax.rem(i, 2))
            return (low + lax.div(i, 2)) * (1 - 2 * lax.rem(i, 2))

        def multiply(i):
            block = zmod(z + offset(i))
            k = emod(block - e)
            w = WO[block]
            XS[k] = dot(G[span(o, TL), :], w).astype(BF16)
            swap(k).start()
            MO[k] = dot(G[span(c, TL), :], w)

        each(0, total, multiply)

        def reduce(i):
            k = emod(zmod(z + offset(i)) - e)
            swap(k).wait_recv()
            both = (MO[k] + XR[k].astype(F32)).astype(BF16)
            OS[k] = both

            @pl.when(k > 0)
            def _():
                out_send(k).start()

        each(0, total, reduce)

    if H > 5:
        pump(H + 3)
        group(0, 3)
        pump(H + 5)
        group(4, 5)
        pump(2 * H)
        group(6, H)
    else:
        pump(2 * H)
        group(0, H)
    result = OS[0].astype(F32)
    for k in range(1, NE):
        out_send(k).wait_recv()
        result += RO[k].astype(F32)
    out[...] = result.astype(BF16)

    for p in range(3):
        pair(p, c).wait_send()
    halo.wait_send()
    for i in range(near + len(far)):
        state_send(i).wait_send()

    def drain(k):
        tok_send(k).wait_send()
        out_send(k).wait_send()

    each(1, NE, drain)

    def drain_all(k, rel):
        sum_send(k, rel).wait_send()
        all_send(k, rel).wait_send()

    everyone(drain_all)

    def drain_pair(k):
        tok_fwd(k).wait_send()
        swap(k).wait_send()

    each(0, NE, drain_pair)

    def drain_ring(s):
        for p in range(3):
            for d in range(2):
                for h in range(2):
                    hop(p, d, s, h).wait_send()

    each(1, H, drain_ring)
    for p in range(3):
        for h in range(2):
            hop(p, h, H, h).wait_send()


def local(
    tokens, segment_ids, w_in_x, w_in_z, conv_weight, conv_bias, w_xproj, w_dt, dt_bias,
    a_rate, d_skip, w_out,
):
    NE, NZ = lax.axis_size("expert"), lax.axis_size("fsdp") // 2
    TL, DC = tokens.shape
    KR_, C2 = w_in_x.shape
    CH, OC, R, N = C2 // 2, w_out.shape[1], w_dt.shape[0], a_rate.shape[1]
    T, J, H = 2 * TL, TL // 4, NZ // 2
    PW = R + 128
    z = lax.axis_index("fsdp") // 2
    padded = jnp.concatenate([jnp.full((3,), -1, jnp.int32), segment_ids], 0)
    window = lax.dynamic_slice_in_dim(padded, z * T, T + 3)
    same = jnp.stack([window[3 - k : 3 - k + T] == window[3:] for k in (1, 2, 3)])
    masks = same.reshape(3, 8, J).transpose(2, 1, 0).reshape(T, 3).astype(F32)
    masks = jnp.pad(masks, ((0, 0), (0, 125)))
    wxp = jnp.pad(w_xproj, ((0, 0), (0, PW - w_xproj.shape[1])))
    near = min(H, 4)
    rounds = near + H // near - 1
    CR = -(-PW // 256) * 16
    sizes = (NE, NZ, TL, KR_, CH, OC, R, N)
    V = pltpu.VMEM
    dma = pltpu.SemaphoreType.DMA
    any_space = pl.BlockSpec(memory_space=pl.ANY)
    vmem = pl.BlockSpec(memory_space=pltpu.VMEM)
    return pl.pallas_call(
        functools.partial(kernel, sizes),
        out_shape=jax.ShapeDtypeStruct((TL, DC), BF16),
        in_specs=[any_space] * 4 + [vmem] * 8,
        out_specs=vmem,
        scratch_shapes=[
            V((NE, T, DC), BF16),
            V((NZ, 2 * KR_, CH), BF16),
            V((NZ, 2 * KR_, CH), BF16),
            V((NZ, CH, 2 * OC), BF16),
            V((T, CH), F32),
            V((T, CH), F32),
            V((T, CH), F32),
            V((24, CH), F32),
            V((T, CH), F32),
            V((2 * NE, CR, 128), BF16),
            V((2 * NE, CR, 128), BF16),
            V((2 * NE, CR, 128), BF16),
            V((T, PW), F32),
            V((T, CH), F32),
            V((T, CH), F32),
            V((T, CH), F32),
            V((T, CH), F32),
            V((N, 8, CH), F32),
            V((N, 8, CH), F32),
            V((2, 2 * N, CH), BF16),
            V((rounds, 2 * N, CH), BF16),
            V((T, CH), BF16),
            V((NE, TL, DC), BF16),
            V((NE, TL, DC), BF16),
            V((NE, TL, DC), F32),
            V((NE, TL, DC), BF16),
            V((NE, TL, DC), BF16),
            dma((4,)),
            dma((3,)), dma((3,)),
            dma((NE,)), dma((NE,)),
            dma((NE,)), dma((NE,)),
            dma((3, 2, H + 1, 2)), dma((3, 2, H + 1, 2)),
            dma(()), dma(()),
            dma((2, NE)), dma((2, NE)),
            dma((2, NE)), dma((2, NE)),
            dma((rounds,)), dma((rounds,)),
            dma((NE,)), dma((NE,)),
            dma((NE,)), dma((NE,)),
        ],
        compiler_params=pltpu.CompilerParams(
            collective_id=0, has_side_effects=True, vmem_limit_bytes=48 * 1024 * 1024
        ),
    )(
        tokens, w_in_x, w_in_z, w_out, conv_weight, conv_bias[None, :], wxp, w_dt,
        dt_bias[None, :], a_rate.T, d_skip[None, :], masks,
    )


def solution(mesh):
    placed = (
        P("fsdp", "expert"),
        P(),
        P("fsdp", "expert"),
        P("fsdp", "expert"),
        P(None, "expert"),
        P("expert"),
        P("expert", None),
        P(None, "expert"),
        P("expert"),
        P("expert", None),
        P("expert"),
        P("expert", "fsdp"),
    )
    return jax.shard_map(
        local, mesh=mesh, in_specs=placed, out_specs=P("fsdp", "expert"), check_vma=False
    )
```

```python
import functools
import math

import jax
import jax.numpy as jnp
from jax import lax
from jax.experimental import pallas as pl
from jax.experimental.pallas import tpu as pltpu
from jax.sharding import PartitionSpec as P

F32 = jnp.float32
BF16 = jnp.bfloat16
FAR = 1e30
LOG2E = 1.0 / math.log(2.0)
MESH = pl.DeviceIdType.MESH


def silu(v):
    return v * jax.nn.sigmoid(v)


def dot(a, b):
    return jnp.dot(a, b, preferred_element_type=F32)


def kernel(
    sizes,
    tok, wx, wz, wo, conv_w, conv_b, wxp, wdt, dt_bias, rates, d_skip, masks,
    out,
    TOK, WX, WZ, WO, AX, AZ, XP, HALO, XA, PB, RB, GB, PR,
    DD, DX, SC, Y, HE, PE, KM, KR, G, XS, XR, MO, OS, RO,
    local_sem, pair_s, pair_r, tok_s, tok_r, fwd_s, fwd_r, ring_s, ring_r,
    halo_s, halo_r, sum_s, sum_r, all_s, all_r,
    state_s, state_r, swap_s, swap_r, out_s, out_r,
):
    NE, NZ, TL, KR_, CH, OC, R, N = sizes
    T, J, H = 2 * TL, TL // 4, NZ // 2
    L = (R + 128) // 128
    CR = PB.shape[1]
    near = min(H, 4)
    far = [near * i for i in range(1, H // near)]
    e = lax.axis_index("expert")
    f = lax.axis_index("fsdp")
    z = lax.div(f, 2)
    c = lax.rem(f, 2)
    o = 1 - c

    def zmod(v):
        return lax.rem(v + 2 * NZ, NZ)

    def emod(v):
        return lax.rem(v + 2 * NE, NE)

    def at(e_, z_, c_):
        return (e_, 2 * z_ + c_)

    def remote(src, dst, ss, rs, dev):
        return pltpu.make_async_remote_copy(
            src_ref=src, dst_ref=dst, send_sem=ss, recv_sem=rs, device_id=dev, device_id_type=MESH
        )

    def span(i, n):
        return pl.ds(pl.multiple_of(i * n, n), n)

    def each(lo, hi, fn):
        def body(k, _):
            fn(k)
            return 0

        lax.fori_loop(lo, hi, body, 0)

    partner = at(e, z, o)

    own = [
        pltpu.make_async_copy(wx.at[:, span(c, CH)], WX.at[z, span(c, KR_)], local_sem.at[0]),
        pltpu.make_async_copy(wz.at[:, span(c, CH)], WZ.at[z, span(c, KR_)], local_sem.at[1]),
        pltpu.make_async_copy(wo.at[span(c, CH)], WO.at[z, :, span(c, OC)], local_sem.at[2]),
        pltpu.make_async_copy(tok, TOK.at[e, span(c, TL)], local_sem.at[3]),
    ]
    for copy in own:
        copy.start()

    barrier = pltpu.get_barrier_semaphore()

    def greet(dev):
        pl.semaphore_signal(barrier, inc=1, device_id=dev, device_id_type=MESH)

    friends = [partner]
    for d in sorted(set(range(1, near + 1)) | set(far)):
        friends += [at(e, zmod(z + d), c), at(e, zmod(z - d), c)]
    count = 1 + 2 * len(set(range(1, near + 1)) | set(far))
    if near == H and NZ == 2 * H and H < 3:
        friends = friends[:-1]
        count -= 1
    for dev in friends:
        greet(dev)

    def greet_plane(k):
        greet(at(emod(e + k), z, c))
        greet(at(emod(e + k), z, o))

    each(1, NE, greet_plane)
    pl.semaphore_wait(barrier, count + 2 * (NE - 1))

    def pair(p, side):
        src = [wx.at[:, span(o, CH)], wz.at[:, span(o, CH)], wo.at[span(o, CH)]][p]
        dst = [WX.at[z, span(side, KR_)], WZ.at[z, span(side, KR_)], WO.at[z, :, span(side, OC)]][p]
        return remote(src, dst, pair_s.at[p], pair_r.at[p], partner)

    pair(0, c).start()

    stacks = [WX, WZ, WO]

    def piece(p, block, h):
        rows = stacks[p].shape[1] // 2
        return stacks[p].at[block, span(h, rows)]

    def hop(p, d, s, h):
        sign = 1 - 2 * d
        block = zmod(z - sign * (s - 1))
        return remote(
            piece(p, block, h), piece(p, block, h),
            ring_s.at[p, d, s, h], ring_r.at[p, d, s, h], at(e, zmod(z + sign), c),
        )

    def arrive(p, d, s, h):
        sign = 1 - 2 * d
        block = zmod(z - sign * s)
        remote(
            piece(p, block, h), piece(p, block, h),
            ring_s.at[p, d, s, h], ring_r.at[p, d, s, h], at(e, zmod(z + sign), c),
        ).wait_recv()

    own[0].wait()
    hop(0, 0, 1, c).start()
    hop(0, 1, 1, c).start()
    pair(1, c).start()
    pair(2, c).start()

    def tok_send(k):
        return remote(
            tok, TOK.at[e, span(c, TL)], tok_s.at[k], tok_r.at[k], at(emod(e + k), z, c)
        )

    def tok_in(k):
        return remote(
            tok, TOK.at[emod(e - k), span(c, TL)], tok_s.at[k], tok_r.at[k], partner
        )

    def tok_fwd(k):
        b = emod(e - k)
        return remote(
            TOK.at[b, span(c, TL)], TOK.at[b, span(c, TL)], fwd_s.at[k], fwd_r.at[k], partner
        )

    def tok_fwd_in(k):
        b = emod(e - k)
        return remote(
            TOK.at[b, span(o, TL)], TOK.at[b, span(o, TL)], fwd_s.at[k], fwd_r.at[k], partner
        )

    pair(0, o).wait_recv()
    hop(0, 0, 1, o).start()
    hop(0, 1, 1, o).start()
    each(1, NE, lambda k: tok_send(k).start())
    own[3].wait()
    tok_fwd(0).start()

    def begin(p):
        own[p].wait()
        pair(p, o).wait_recv()
        for h in (0, 1):
            for d in (0, 1):
                hop(p, d, 1, h).start()

    def step(p, s):
        for h in (0, 1):
            for d in (0, 1):
                if s < H or d == h:
                    arrive(p, d, s, h)
                    if s < H - 1 or (s == H - 1 and d == h):
                        hop(p, d, s + 1, h).start()

    def add(acc, w, block, first=False):
        product = dot(TOK[block], w[block])
        acc[...] = product if first else acc[...] + product

    def add_step(acc, w, s):
        add(acc, w, zmod(z - s))
        if s < H:
            add(acc, w, zmod(z + s))

    def relay(k):
        tok_in(k).wait_recv()
        tok_fwd(k).start()

    relay_at, tokens_at = min(4, H - 1), min(7, H)
    z_after = {2 * i + 1: i for i in range(1, H) if 2 * i + 1 < H}
    z_done = len(z_after)
    done = 0
    for s in range(1, H + 1):
        step(0, s)
        if s == 1:
            begin(1)
        if s in z_after:
            step(1, z_after[s])
        if s == H - 1:
            begin(2)
        if s == relay_at:
            each(1, NE, relay)
        if s == tokens_at:
            each(0, NE, lambda k: tok_fwd_in(k).wait_recv())
            add(AX, WX, z, first=True)
        if s >= tokens_at:
            for s_ in range(done + 1, s):
                add_step(AX, WX, s_)
            done = s - 1
    add_step(AX, WX, H)

    position = [0]

    def pump(upto):
        while position[0] < min(upto, H):
            position[0] += 1
            s = position[0]
            if s + z_done <= H:
                step(1, s + z_done)
            step(2, s)
            if s == 1:
                add(AZ, WZ, z, first=True)
                for i in range(1, z_done + 1):
                    add_step(AZ, WZ, i)
            if s + z_done <= H:
                add_step(AZ, WZ, s + z_done)

    row = lax.broadcasted_iota(jnp.int32, (T, T), 0)
    col = lax.broadcasted_iota(jnp.int32, (T, T), 1)
    perm = (col == lax.rem(row, 8) * J + lax.div(row, 8)).astype(F32).astype(BF16)
    XP[...] = dot(perm, AX[...].astype(BF16))
    rim = XP.at[pl.ds((J - 3) * 8, 24)]
    halo = remote(rim, HALO, halo_s, halo_r, at(e, zmod(z + 1), c))
    halo.start()
    halo.wait_recv()
    lane_c = span(c, CH)
    top = lax.broadcasted_iota(jnp.int32, (8, CH), 0) == 0
    early = []
    for i in range(3):
        mine = pltpu.roll(XP[(J - 3 + i) * 8 : (J - 2 + i) * 8], 1, 0)
        theirs = pltpu.roll(HALO[i * 8 : (i + 1) * 8], 1, 0)
        early.append(jnp.where(top, theirs, mine))
    ext = jnp.concatenate(early + [XP[...]], 0)
    conv = conv_b[:, lane_c] + conv_w[3:4, lane_c] * ext[24:]
    for k in range(1, 4):
        conv += conv_w[3 - k : 4 - k, lane_c] * ext[24 - 8 * k : 24 - 8 * k + T] * masks[:, k - 1 : k]
    x_act = silu(conv).astype(BF16)
    XA[...] = x_act.astype(F32)
    PR[...] = dot(x_act, wxp[span(c, CH), :])

    pump(1)
    blank = [jnp.zeros((CR - 8 * L, 128), F32)] if CR > 8 * L else []

    def pack(q):
        rows = span(q, 8)
        tiles = [PR[rows, l * 128 : (l + 1) * 128] for l in range(L)]
        PB[q] = jnp.concatenate(tiles + blank, 0).astype(BF16)

    each(0, 2 * NE, pack)

    def plane(k, rel):
        core = c if rel == 0 else o
        return emod(e + k), core

    def sum_send(k, rel):
        e_, core = plane(k, rel)
        return remote(
            PB.at[core * NE + e_], RB.at[rel * NE + k],
            sum_s.at[rel, k], sum_r.at[rel, k], at(e_, z, core),
        )

    mine = c * NE + e

    def all_send(k, rel):
        e_, core = plane(k, rel)
        return remote(
            GB.at[mine], GB.at[mine], all_s.at[rel, k], all_r.at[rel, k], at(e_, z, core)
        )

    def all_in(k, rel):
        e_, core = plane(-k, rel)
        theirs = core * NE + e_
        return remote(
            GB.at[theirs], GB.at[theirs], all_s.at[rel, k], all_r.at[rel, k], at(e_, z, core)
        )

    def everyone(fn):
        fn(0, 1)

        def both(k):
            fn(k, 1)
            fn(k, 0)

        each(1, NE, both)

    everyone(lambda k, rel: sum_send(k, rel).start())
    pump(2)
    everyone(lambda k, rel: sum_send(k, rel).wait_recv())
    total = PB[mine].astype(F32)
    for k in range(1, 2 * NE):
        total += RB[k].astype(F32)
    GB[mine] = total.astype(BF16)
    everyone(lambda k, rel: all_send(k, rel).start())
    pump(3)
    everyone(lambda k, rel: all_in(k, rel).wait_recv())

    def unpack(q):
        chunk = GB[q].astype(F32)
        for l in range(L):
            PR[span(q, 8), l * 128 : (l + 1) * 128] = chunk[8 * l : 8 * l + 8]

    each(0, 2 * NE, unpack)
    pump(4)
    delta = dot(PR[:, :R].astype(BF16), wdt[:, lane_c]) + dt_bias[:, lane_c]
    delta = jnp.maximum(delta, 0.0) + jnp.log1p(jnp.exp(-jnp.abs(delta)))
    DX[...] = delta * XA[...]
    DD[...] = delta + (1.0 - masks[:, 0:1]) * FAR

    slope = [rates[n : n + 1, lane_c] * (-LOG2E) for n in range(N)]

    def forward(j, carry):
        hs, reach = carry
        r = pl.ds(pl.multiple_of(j * 8, 8), 8)
        dd, dx, bc = DD[r, :], DX[r, :], PR[r, R : R + 128]
        reach = reach + dd
        SC[r, :] = reach
        y = jnp.zeros((8, CH), F32)
        later = []
        for n in range(N):
            h = jnp.exp2(dd * slope[n]) * hs[n] + dx * bc[:, n : n + 1]
            y = y + h * bc[:, N + n : N + n + 1]
            later.append(h)
        Y[r, :] = y
        return later, reach

    zero = jnp.zeros((8, CH), F32)
    ends, reach = lax.fori_loop(0, J, forward, ([zero] * N, zero))
    sub = lax.broadcasted_iota(jnp.int32, (8, CH), 0)
    states = []
    for n in range(N):
        h, p = ends[n], jnp.exp2(reach * slope[n])
        for d in (1, 2, 4):
            before = sub >= d
            h = h + p * jnp.where(before, pltpu.roll(h, d, 0), 0.0)
            p = p * jnp.where(before, pltpu.roll(p, d, 0), 1.0)
        HE[n] = jnp.where(top, 0.0, pltpu.roll(h, 1, 0))
        PE[n] = jnp.where(top, 1.0, pltpu.roll(p, 1, 0))
        states.append(h[7:8])
    span_sum = jnp.broadcast_to(jnp.sum(reach, axis=0, keepdims=True), (N, CH))
    KM[0] = jnp.concatenate(states + [span_sum], 0).astype(BF16)

    steep = rates[:, lane_c] * (-LOG2E)

    def state_send(i):
        d = i + 1 if i < near else far[i - near]
        return remote(
            KM.at[0 if i < near else 1], KR.at[i], state_s.at[i], state_r.at[i],
            at(e, zmod(z + d), c),
        )

    def join(earlier, latter):
        both = latter.astype(F32)
        h, reach = both[:N], both[N:]
        if earlier is None:
            return h, reach
        return jnp.exp2(reach * steep) * earlier[0] + h, earlier[1] + reach

    for i in range(near):
        state_send(i).start()
    pump(5)
    for i in range(near):
        state_send(i).wait_recv()
    entering = None
    for i in range(near - 1, -1, -1):
        entering = join(entering, KR[i])
    if far:
        KM[1] = jnp.concatenate(entering, 0).astype(BF16)
        for i in range(near, near + len(far)):
            state_send(i).start()
        pump(6)
        for i in range(near, near + len(far)):
            state_send(i).wait_recv()
        combined = None
        for i in range(near + len(far) - 1, near - 1, -1):
            combined = join(combined, KR[i])
        entering = join(combined, KM[1])
    pump(7)
    for n in range(N):
        HE[n] = HE[n] + PE[n] * entering[0][n : n + 1, :]

    def correct(j, _):
        r = pl.ds(pl.multiple_of(j * 8, 8), 8)
        reach, bc = SC[r, :], PR[r, R : R + 128]
        y = Y[r, :]
        for n in range(N):
            y = y + jnp.exp2(reach * slope[n]) * HE[n] * bc[:, N + n : N + n + 1]
        Y[r, :] = y + d_skip[:, lane_c] * XA[r, :]
        return 0

    lax.fori_loop(0, J, correct, 0)
    back = (col == lax.rem(row, J) * 8 + lax.div(row, J)).astype(F32).astype(BF16)
    pump(H)
    gate = silu(dot(perm, AZ[...].astype(BF16)))
    G[...] = dot(back, (Y[...] * gate).astype(BF16)).astype(BF16)

    def swap(k):
        return remote(XS.at[k], XR.at[k], swap_s.at[k], swap_r.at[k], partner)

    def out_send(k):
        return remote(OS.at[k], RO.at[k], out_s.at[k], out_r.at[k], at(emod(e + k), z, c))

    def group(low, high):
        total = 2 * (high - low + 1) - (low == 0) - (high == H)

        def offset(i):
            i = lax.rem(i + e, total)
            if low == 0:
                return lax.div(i + 1, 2) * (1 - 2 * lax.rem(i, 2))
            return (low + lax.div(i, 2)) * (1 - 2 * lax.rem(i, 2))

        def multiply(i):
            block = zmod(z + offset(i))
            k = emod(block - e)
            w = WO[block]
            XS[k] = dot(G[span(o, TL), :], w).astype(BF16)
            swap(k).start()
            MO[k] = dot(G[span(c, TL), :], w)

        def reduce(i):
            k = emod(zmod(z + offset(i)) - e)
            swap(k).wait_recv()
            OS[k] = (MO[k] + XR[k].astype(F32)).astype(BF16)

            @pl.when(k > 0)
            def _():
                out_send(k).start()

        ahead = min(3, total)
        each(0, ahead, multiply)

        def both(i):
            multiply(i)
            reduce(i - ahead)

        each(ahead, total, both)
        each(total - ahead, total, reduce)

    group(0, H)
    result = OS[0].astype(F32)
    for k in range(1, NE):
        out_send(k).wait_recv()
        result += RO[k].astype(F32)
    out[...] = result.astype(BF16)

    for p in range(3):
        pair(p, c).wait_send()
    halo.wait_send()
    for i in range(near + len(far)):
        state_send(i).wait_send()

    def drain(k):
        tok_send(k).wait_send()
        out_send(k).wait_send()

    each(1, NE, drain)

    def drain_all(k, rel):
        sum_send(k, rel).wait_send()
        all_send(k, rel).wait_send()

    everyone(drain_all)

    def drain_pair(k):
        tok_fwd(k).wait_send()
        swap(k).wait_send()

    each(0, NE, drain_pair)

    def drain_ring(s):
        for p in range(3):
            for d in range(2):
                for h in range(2):
                    hop(p, d, s, h).wait_send()

    each(1, H, drain_ring)
    for p in range(3):
        for h in range(2):
            hop(p, h, H, h).wait_send()


def local(
    tokens, segment_ids, w_in_x, w_in_z, conv_weight, conv_bias, w_xproj, w_dt, dt_bias,
    a_rate, d_skip, w_out,
):
    NE, NZ = lax.axis_size("expert"), lax.axis_size("fsdp") // 2
    TL, DC = tokens.shape
    KR_, C2 = w_in_x.shape
    CH, OC, R, N = C2 // 2, w_out.shape[1], w_dt.shape[0], a_rate.shape[1]
    T, J, H = 2 * TL, TL // 4, NZ // 2
    PW = R + 128
    z = lax.axis_index("fsdp") // 2
    padded = jnp.concatenate([jnp.full((3,), -1, jnp.int32), segment_ids], 0)
    window = lax.dynamic_slice_in_dim(padded, z * T, T + 3)
    same = jnp.stack([window[3 - k : 3 - k + T] == window[3:] for k in (1, 2, 3)])
    masks = same.reshape(3, 8, J).transpose(2, 1, 0).reshape(T, 3).astype(F32)
    masks = jnp.pad(masks, ((0, 0), (0, 125)))
    wxp = jnp.pad(w_xproj, ((0, 0), (0, PW - w_xproj.shape[1])))
    near = min(H, 4)
    rounds = near + H // near - 1
    CR = -(-PW // 256) * 16
    sizes = (NE, NZ, TL, KR_, CH, OC, R, N)
    V = pltpu.VMEM
    dma = pltpu.SemaphoreType.DMA
    any_space = pl.BlockSpec(memory_space=pl.ANY)
    vmem = pl.BlockSpec(memory_space=pltpu.VMEM)
    return pl.pallas_call(
        functools.partial(kernel, sizes),
        out_shape=jax.ShapeDtypeStruct((TL, DC), BF16),
        in_specs=[any_space] * 4 + [vmem] * 8,
        out_specs=vmem,
        scratch_shapes=[
            V((NE, T, DC), BF16),
            V((NZ, 2 * KR_, CH), BF16),
            V((NZ, 2 * KR_, CH), BF16),
            V((NZ, CH, 2 * OC), BF16),
            V((T, CH), F32),
            V((T, CH), F32),
            V((T, CH), F32),
            V((24, CH), F32),
            V((T, CH), F32),
            V((2 * NE, CR, 128), BF16),
            V((2 * NE, CR, 128), BF16),
            V((2 * NE, CR, 128), BF16),
            V((T, PW), F32),
            V((T, CH), F32),
            V((T, CH), F32),
            V((T, CH), F32),
            V((T, CH), F32),
            V((N, 8, CH), F32),
            V((N, 8, CH), F32),
            V((2, 2 * N, CH), BF16),
            V((rounds, 2 * N, CH), BF16),
            V((T, CH), BF16),
            V((NE, TL, DC), BF16),
            V((NE, TL, DC), BF16),
            V((NE, TL, DC), F32),
            V((NE, TL, DC), BF16),
            V((NE, TL, DC), BF16),
            dma((4,)),
            dma((3,)), dma((3,)),
            dma((NE,)), dma((NE,)),
            dma((NE,)), dma((NE,)),
            dma((3, 2, H + 1, 2)), dma((3, 2, H + 1, 2)),
            dma(()), dma(()),
            dma((2, NE)), dma((2, NE)),
            dma((2, NE)), dma((2, NE)),
            dma((rounds,)), dma((rounds,)),
            dma((NE,)), dma((NE,)),
            dma((NE,)), dma((NE,)),
        ],
        compiler_params=pltpu.CompilerParams(
            collective_id=0, has_side_effects=True, vmem_limit_bytes=48 * 1024 * 1024
        ),
    )(
        tokens, w_in_x, w_in_z, w_out, conv_weight, conv_bias[None, :], wxp, w_dt,
        dt_bias[None, :], a_rate.T, d_skip[None, :], masks,
    )


def solution(mesh):
    placed = (
        P("fsdp", "expert"),
        P(),
        P("fsdp", "expert"),
        P("fsdp", "expert"),
        P(None, "expert"),
        P("expert"),
        P("expert", None),
        P(None, "expert"),
        P("expert"),
        P("expert", None),
        P("expert"),
        P("expert", "fsdp"),
    )
    return jax.shard_map(
        local, mesh=mesh, in_specs=placed, out_specs=P("fsdp", "expert"), check_vma=False
    )
```

```python
import functools
import math

import jax
import jax.numpy as jnp
from jax import lax
from jax.experimental import pallas as pl
from jax.experimental.pallas import tpu as pltpu
from jax.sharding import PartitionSpec as P

F32 = jnp.float32
BF16 = jnp.bfloat16
FAR = 1e30
LOG2E = 1.0 / math.log(2.0)
MESH = pl.DeviceIdType.MESH


def silu(v):
    return v * jax.nn.sigmoid(v)


def dot(a, b):
    return jnp.dot(a, b, preferred_element_type=F32)


def kernel(
    sizes,
    tok, wx, wz, wo, conv_w, conv_b, wxp, wdt, dt_bias, rates, d_skip, ids,
    out,
    TOK, WX, WZ, WO, WP, AX, AZ, XP, HALO, XA, PB, RB, GB, PR,
    DD, DX, SC, Y, HE, PE, KM, KR, KS, SR, MASK, PERM, G, GP, MO, OS, RO,
    local_sem, pair_s, pair_r, tok_s, tok_r, fwd_s, fwd_r, ring_s, ring_r,
    halo_s, halo_r, sum_s, sum_r, all_s, all_r,
    state_s, state_r, reach_s, reach_r, gate_s, gate_r, rest_s, rest_r, out_s, out_r,
):
    NE, NZ, TL, KR_, CH, OC, R, N = sizes
    T, J, H = 2 * TL, TL // 4, NZ // 2
    L = (R + 128) // 128
    CR = PB.shape[1]
    near = min(H, 4)
    far = [near * i for i in range(1, H // near)]
    e = lax.axis_index("expert")
    f = lax.axis_index("fsdp")
    z = lax.div(f, 2)
    c = lax.rem(f, 2)
    o = 1 - c

    def zmod(v):
        return lax.rem(v + 2 * NZ, NZ)

    def emod(v):
        return lax.rem(v + 2 * NE, NE)

    def at(e_, z_, c_):
        return (e_, 2 * z_ + c_)

    def remote(src, dst, ss, rs, dev):
        return pltpu.make_async_remote_copy(
            src_ref=src, dst_ref=dst, send_sem=ss, recv_sem=rs, device_id=dev, device_id_type=MESH
        )

    def span(i, n):
        return pl.ds(pl.multiple_of(i * n, n), n)

    def each(lo, hi, fn):
        def body(k, _):
            fn(k)
            return 0

        lax.fori_loop(lo, hi, body, 0)

    partner = at(e, z, o)

    own = [
        pltpu.make_async_copy(wx.at[:, span(c, CH)], WX.at[z, span(c, KR_)], local_sem.at[0]),
        pltpu.make_async_copy(wz.at[:, span(c, CH)], WZ.at[z, span(c, KR_)], local_sem.at[1]),
        pltpu.make_async_copy(wo.at[span(c, CH)], WO.at[z, :, span(c, OC)], local_sem.at[2]),
        pltpu.make_async_copy(tok, TOK.at[e, span(c, TL)], local_sem.at[3]),
    ]
    for copy in own:
        copy.start()

    row = lax.broadcasted_iota(jnp.int32, (T, T), 0)
    col = lax.broadcasted_iota(jnp.int32, (T, T), 1)
    PERM[...] = (col == lax.rem(row, 8) * J + lax.div(row, 8)).astype(F32).astype(BF16)

    here = jnp.broadcast_to(ids[pl.ds(z, 1), :], (8, T))
    previous = jnp.broadcast_to(ids[pl.ds(zmod(z - 1), 1), :], (8, T))
    lane = lax.broadcasted_iota(jnp.int32, (8, T), 1)
    line = lax.broadcasted_iota(jnp.int32, (8, T), 0)
    same = jnp.zeros((8, T), F32)
    for k in range(1, 4):
        shifted = jnp.where(lane >= k, pltpu.roll(here, k, 1), pltpu.roll(previous, k, 1))
        inside = lane + z * T >= k
        same = jnp.where((line == k - 1) & inside & (shifted == here), 1.0, same)
    MASK[...] = lax.dot_general(
        PERM[...], same.astype(BF16), (((1,), (1,)), ((), ())), preferred_element_type=F32
    )

    barrier = pltpu.get_barrier_semaphore()

    def greet(dev):
        pl.semaphore_signal(barrier, inc=1, device_id=dev, device_id_type=MESH)

    friends = [partner]
    for d in sorted(set(range(1, near + 1)) | set(far)):
        friends += [at(e, zmod(z + d), c), at(e, zmod(z - d), c)]
    count = 1 + 2 * len(set(range(1, near + 1)) | set(far))
    if near == H and NZ == 2 * H and H < 3:
        friends = friends[:-1]
        count -= 1
    for dev in friends:
        greet(dev)

    def greet_plane(k):
        greet(at(emod(e + k), z, c))
        greet(at(emod(e + k), z, o))

    each(1, NE, greet_plane)
    pl.semaphore_wait(barrier, count + 2 * (NE - 1))

    def pair(p, side):
        src = [wx.at[:, span(o, CH)], wz.at[:, span(o, CH)], wo.at[span(o, CH)]][p]
        dst = [WX.at[z, span(side, KR_)], WZ.at[z, span(side, KR_)], WO.at[z, :, span(side, OC)]][p]
        return remote(src, dst, pair_s.at[p], pair_r.at[p], partner)

    pair(0, c).start()

    stacks = [WX, WZ, WO]

    def piece(p, block, h):
        rows = stacks[p].shape[1] // 2
        return stacks[p].at[block, span(h, rows)]

    def hop(p, d, s, h):
        sign = 1 - 2 * d
        block = zmod(z - sign * (s - 1))
        return remote(
            piece(p, block, h), piece(p, block, h),
            ring_s.at[p, d, s, h], ring_r.at[p, d, s, h], at(e, zmod(z + sign), c),
        )

    def arrive(p, d, s, h):
        sign = 1 - 2 * d
        block = zmod(z - sign * s)
        remote(
            piece(p, block, h), piece(p, block, h),
            ring_s.at[p, d, s, h], ring_r.at[p, d, s, h], at(e, zmod(z + sign), c),
        ).wait_recv()

    own[0].wait()
    hop(0, 0, 1, c).start()
    hop(0, 1, 1, c).start()
    pair(1, c).start()
    pair(2, c).start()

    def tok_send(k):
        return remote(
            tok, TOK.at[e, span(c, TL)], tok_s.at[k], tok_r.at[k], at(emod(e + k), z, c)
        )

    def tok_in(k):
        return remote(
            tok, TOK.at[emod(e - k), span(c, TL)], tok_s.at[k], tok_r.at[k], partner
        )

    def tok_fwd(k):
        b = emod(e - k)
        return remote(
            TOK.at[b, span(c, TL)], TOK.at[b, span(c, TL)], fwd_s.at[k], fwd_r.at[k], partner
        )

    def tok_fwd_in(k):
        b = emod(e - k)
        return remote(
            TOK.at[b, span(o, TL)], TOK.at[b, span(o, TL)], fwd_s.at[k], fwd_r.at[k], partner
        )

    pair(0, o).wait_recv()
    hop(0, 0, 1, o).start()
    hop(0, 1, 1, o).start()
    each(1, NE, lambda k: tok_send(k).start())
    own[3].wait()
    tok_fwd(0).start()

    def begin(p):
        own[p].wait()
        pair(p, o).wait_recv()
        for h in (0, 1):
            for d in (0, 1):
                hop(p, d, 1, h).start()

    def rest(d, s):
        block = zmod(z - (1 - 2 * d) * s)
        return remote(WO.at[block], WP.at[block], rest_s.at[d, s], rest_r.at[d, s], partner)

    rests = [(0, s) for s in range(H + 1)] + [(1, s) for s in range(1, H)]

    def step(p, s):
        for h in (0, 1):
            for d in (0, 1):
                if s < H or d == h:
                    arrive(p, d, s, h)
                    if s < H - 1 or (s == H - 1 and d == h):
                        hop(p, d, s + 1, h).start()
        if p == 2:
            for d in range(2 if s < H else 1):
                rest(d, s).start()

    def add(acc, w, block, first=False):
        product = dot(TOK[block], w[block])
        acc[...] = product if first else acc[...] + product

    def add_step(acc, w, s):
        add(acc, w, zmod(z - s))
        if s < H:
            add(acc, w, zmod(z + s))

    def relay(k):
        tok_in(k).wait_recv()
        tok_fwd(k).start()

    relay_at, tokens_at = min(4, H - 1), min(7, H)
    z_after = {2 * i + 1: i for i in range(1, H) if 2 * i + 1 < H}
    z_done = len(z_after)
    done = 0
    for s in range(1, H + 1):
        step(0, s)
        if s == 1:
            begin(1)
        if s in z_after:
            step(1, z_after[s])
        if s == H - 1:
            begin(2)
            rest(0, 0).start()
        if s == relay_at:
            each(1, NE, relay)
        if s == tokens_at:
            each(0, NE, lambda k: tok_fwd_in(k).wait_recv())
            add(AX, WX, z, first=True)
        if s >= tokens_at:
            for s_ in range(done + 1, s):
                add_step(AX, WX, s_)
            done = s - 1
    add_step(AX, WX, H)

    position = [0]

    def pump(upto):
        while position[0] < min(upto, H):
            position[0] += 1
            s = position[0]
            if s + z_done <= H:
                step(1, s + z_done)
            step(2, s)
            if s == 1:
                add(AZ, WZ, z, first=True)
                for i in range(1, z_done + 1):
                    add_step(AZ, WZ, i)
            if s + z_done <= H:
                add_step(AZ, WZ, s + z_done)

    perm = PERM[...]
    XP[...] = dot(perm, AX[...].astype(BF16))
    rim = XP.at[pl.ds((J - 3) * 8, 24)]
    halo = remote(rim, HALO, halo_s, halo_r, at(e, zmod(z + 1), c))
    halo.start()
    halo.wait_recv()
    lane_c = span(c, CH)
    top = lax.broadcasted_iota(jnp.int32, (8, CH), 0) == 0
    early = []
    for i in range(3):
        mine = pltpu.roll(XP[(J - 3 + i) * 8 : (J - 2 + i) * 8], 1, 0)
        theirs = pltpu.roll(HALO[i * 8 : (i + 1) * 8], 1, 0)
        early.append(jnp.where(top, theirs, mine))
    ext = jnp.concatenate(early + [XP[...]], 0)
    conv = conv_b[:, lane_c] + conv_w[3:4, lane_c] * ext[24:]
    for k in range(1, 4):
        conv += conv_w[3 - k : 4 - k, lane_c] * ext[24 - 8 * k : 24 - 8 * k + T] * MASK[:, k - 1 : k]
    x_act = silu(conv).astype(BF16)
    XA[...] = x_act.astype(F32)
    PR[...] = dot(x_act, wxp[span(c, CH), :])

    pump(1)
    blank = [jnp.zeros((CR - 8 * L, 128), F32)] if CR > 8 * L else []

    def pack(q):
        rows = span(q, 8)
        tiles = [PR[rows, l * 128 : (l + 1) * 128] for l in range(L)]
        PB[q] = jnp.concatenate(tiles + blank, 0).astype(BF16)

    each(0, 2 * NE, pack)

    def plane(k, rel):
        core = c if rel == 0 else o
        return emod(e + k), core

    def sum_send(k, rel):
        e_, core = plane(k, rel)
        return remote(
            PB.at[core * NE + e_], RB.at[rel * NE + k],
            sum_s.at[rel, k], sum_r.at[rel, k], at(e_, z, core),
        )

    mine = c * NE + e

    def all_send(k, rel):
        e_, core = plane(k, rel)
        return remote(
            GB.at[mine], GB.at[mine], all_s.at[rel, k], all_r.at[rel, k], at(e_, z, core)
        )

    def all_in(k, rel):
        e_, core = plane(-k, rel)
        theirs = core * NE + e_
        return remote(
            GB.at[theirs], GB.at[theirs], all_s.at[rel, k], all_r.at[rel, k], at(e_, z, core)
        )

    def everyone(fn):
        fn(0, 1)

        def both(k):
            fn(k, 1)
            fn(k, 0)

        each(1, NE, both)

    everyone(lambda k, rel: sum_send(k, rel).start())
    pump(2)
    everyone(lambda k, rel: sum_send(k, rel).wait_recv())
    total = PB[mine].astype(F32)
    for k in range(1, 2 * NE):
        total += RB[k].astype(F32)
    GB[mine] = total.astype(BF16)
    everyone(lambda k, rel: all_send(k, rel).start())
    pump(3)
    everyone(lambda k, rel: all_in(k, rel).wait_recv())

    def unpack(q):
        chunk = GB[q].astype(F32)
        for l in range(L):
            PR[span(q, 8), l * 128 : (l + 1) * 128] = chunk[8 * l : 8 * l + 8]

    each(0, 2 * NE, unpack)
    pump(4)
    delta = dot(PR[:, :R].astype(BF16), wdt[:, lane_c]) + dt_bias[:, lane_c]
    delta = jnp.maximum(delta, 0.0) + jnp.log1p(jnp.exp(-jnp.abs(delta)))
    DX[...] = delta * XA[...]
    DD[...] = delta + (1.0 - MASK[:, 0:1]) * FAR

    def reach_send(i):
        return remote(KS, SR.at[i], reach_s.at[i], reach_r.at[i], at(e, zmod(z + i + 1), c))

    reach_sum = jnp.zeros((8, CH), F32)
    for j in range(J):
        reach_sum += DD[8 * j : 8 * j + 8, :]
    KS[...] = jnp.broadcast_to(jnp.sum(reach_sum, axis=0, keepdims=True), (N, CH)).astype(BF16)
    for i in range(near):
        reach_send(i).start()

    slope = [rates[n : n + 1, lane_c] * (-LOG2E) for n in range(N)]

    def forward(j, carry):
        hs, reach = carry
        r = pl.ds(pl.multiple_of(j * 8, 8), 8)
        dd, dx, bc = DD[r, :], DX[r, :], PR[r, R : R + 128]
        reach = reach + dd
        SC[r, :] = reach
        y = jnp.zeros((8, CH), F32)
        later = []
        for n in range(N):
            h = jnp.exp2(dd * slope[n]) * hs[n] + dx * bc[:, n : n + 1]
            y = y + h * bc[:, N + n : N + n + 1]
            later.append(h)
        Y[r, :] = y
        return later, reach

    zero = jnp.zeros((8, CH), F32)
    ends, reach = lax.fori_loop(0, J, forward, ([zero] * N, zero))
    sub = lax.broadcasted_iota(jnp.int32, (8, CH), 0)
    states = []
    for n in range(N):
        h, p = ends[n], jnp.exp2(reach * slope[n])
        for d in (1, 2, 4):
            before = sub >= d
            h = h + p * jnp.where(before, pltpu.roll(h, d, 0), 0.0)
            p = p * jnp.where(before, pltpu.roll(p, d, 0), 1.0)
        HE[n] = jnp.where(top, 0.0, pltpu.roll(h, 1, 0))
        PE[n] = jnp.where(top, 1.0, pltpu.roll(p, 1, 0))
        states.append(h[7:8])
    KM[0] = jnp.concatenate(states, 0).astype(BF16)

    steep = rates[:, lane_c] * (-LOG2E)

    def state_send(i):
        d = i + 1 if i < near else far[i - near]
        return remote(
            KM.at[0 if i < near else 1], KR.at[i], state_s.at[i], state_r.at[i],
            at(e, zmod(z + d), c),
        )

    for i in range(near):
        state_send(i).start()
    pump(5)
    distance = jnp.zeros((N, CH), F32)
    for i in range(near):
        reach_send(i).wait_recv()
        state_send(i).wait_recv()
    entering = KR[near - 1].astype(F32)
    for i in range(near - 2, -1, -1):
        entering = jnp.exp2(SR[i].astype(F32) * steep) * entering + KR[i].astype(F32)
    for i in range(near):
        distance += SR[i].astype(F32)
    if far:
        KM[1] = entering.astype(BF16)
        state_send(near).start()
        pump(6)
        state_send(near).wait_recv()
        entering = jnp.exp2(distance * steep) * KR[near].astype(F32) + entering
    pump(7)
    for n in range(N):
        HE[n] = HE[n] + PE[n] * entering[n : n + 1, :]

    def correct(j, _):
        r = pl.ds(pl.multiple_of(j * 8, 8), 8)
        reach, bc = SC[r, :], PR[r, R : R + 128]
        y = Y[r, :]
        for n in range(N):
            y = y + jnp.exp2(reach * slope[n]) * HE[n] * bc[:, N + n : N + n + 1]
        Y[r, :] = y + d_skip[:, lane_c] * XA[r, :]
        return 0

    lax.fori_loop(0, J, correct, 0)
    back = (col == lax.rem(row, J) * 8 + lax.div(row, J)).astype(F32).astype(BF16)
    pump(H)
    gate = silu(dot(perm, AZ[...].astype(BF16)))
    G[...] = dot(back, (Y[...] * gate).astype(BF16)).astype(BF16)

    gated = remote(G.at[span(o, TL)], GP, gate_s, gate_r, partner)
    gated.start()

    def out_send(k):
        return remote(OS.at[k], RO.at[k], out_s.at[k], out_r.at[k], at(emod(e + k), z, c))

    def block_at(k):
        return zmod(e + k)

    def multiply(k):
        MO[k] = dot(G[span(c, TL), :], WO[block_at(k)])

    each(0, NE, multiply)
    for d, s in rests:
        rest(d, s).wait_recv()
    gated.wait_recv()

    def finish(k):
        OS[k] = (MO[k] + dot(GP[...], WP[block_at(k)])).astype(BF16)

    def finish_send(k):
        finish(k)
        out_send(k).start()

    each(1, NE, finish_send)
    finish(0)
    result = OS[0].astype(F32)
    for k in range(1, NE):
        out_send(k).wait_recv()
        result += RO[k].astype(F32)
    out[...] = result.astype(BF16)

    for p in range(3):
        pair(p, c).wait_send()
    halo.wait_send()
    for i in range(near + len(far)):
        state_send(i).wait_send()
    for i in range(near):
        reach_send(i).wait_send()

    def drain(k):
        tok_send(k).wait_send()
        out_send(k).wait_send()

    each(1, NE, drain)

    def drain_all(k, rel):
        sum_send(k, rel).wait_send()
        all_send(k, rel).wait_send()

    everyone(drain_all)

    each(0, NE, lambda k: tok_fwd(k).wait_send())
    gated.wait_send()
    for d, s in rests:
        rest(d, s).wait_send()

    def drain_ring(s):
        for p in range(3):
            for d in range(2):
                for h in range(2):
                    hop(p, d, s, h).wait_send()

    each(1, H, drain_ring)
    for p in range(3):
        for h in range(2):
            hop(p, h, H, h).wait_send()


def local(
    tokens, segment_ids, w_in_x, w_in_z, conv_weight, conv_bias, w_xproj, w_dt, dt_bias,
    a_rate, d_skip, w_out,
):
    NE, NZ = lax.axis_size("expert"), lax.axis_size("fsdp") // 2
    TL, DC = tokens.shape
    KR_, C2 = w_in_x.shape
    CH, OC, R, N = C2 // 2, w_out.shape[1], w_dt.shape[0], a_rate.shape[1]
    T, J, H = 2 * TL, TL // 4, NZ // 2
    PW = R + 128
    wxp = jnp.pad(w_xproj, ((0, 0), (0, PW - w_xproj.shape[1])))
    near = min(H, 4)
    rounds = near + H // near - 1
    CR = -(-PW // 256) * 16
    sizes = (NE, NZ, TL, KR_, CH, OC, R, N)
    V = pltpu.VMEM
    dma = pltpu.SemaphoreType.DMA
    any_space = pl.BlockSpec(memory_space=pl.ANY)
    vmem = pl.BlockSpec(memory_space=pltpu.VMEM)
    return pl.pallas_call(
        functools.partial(kernel, sizes),
        out_shape=jax.ShapeDtypeStruct((TL, DC), BF16),
        in_specs=[any_space] * 4 + [vmem] * 8,
        out_specs=vmem,
        scratch_shapes=[
            V((NE, T, DC), BF16),
            V((NZ, 2 * KR_, CH), BF16),
            V((NZ, 2 * KR_, CH), BF16),
            V((NZ, CH, 2 * OC), BF16),
            V((NZ, CH, 2 * OC), BF16),
            V((T, CH), F32),
            V((T, CH), F32),
            V((T, CH), F32),
            V((24, CH), F32),
            V((T, CH), F32),
            V((2 * NE, CR, 128), BF16),
            V((2 * NE, CR, 128), BF16),
            V((2 * NE, CR, 128), BF16),
            V((T, PW), F32),
            V((T, CH), F32),
            V((T, CH), F32),
            V((T, CH), F32),
            V((T, CH), F32),
            V((N, 8, CH), F32),
            V((N, 8, CH), F32),
            V((2, N, CH), BF16),
            V((rounds, N, CH), BF16),
            V((N, CH), BF16),
            V((near, N, CH), BF16),
            V((T, 8), F32),
            V((T, T), BF16),
            V((T, CH), BF16),
            V((TL, CH), BF16),
            V((NE, TL, DC), F32),
            V((NE, TL, DC), BF16),
            V((NE, TL, DC), BF16),
            dma((4,)),
            dma((3,)), dma((3,)),
            dma((NE,)), dma((NE,)),
            dma((NE,)), dma((NE,)),
            dma((3, 2, H + 1, 2)), dma((3, 2, H + 1, 2)),
            dma(()), dma(()),
            dma((2, NE)), dma((2, NE)),
            dma((2, NE)), dma((2, NE)),
            dma((rounds,)), dma((rounds,)),
            dma((near,)), dma((near,)),
            dma(()), dma(()),
            dma((2, H + 1)), dma((2, H + 1)),
            dma((NE,)), dma((NE,)),
        ],
        compiler_params=pltpu.CompilerParams(
            collective_id=0, has_side_effects=True, vmem_limit_bytes=48 * 1024 * 1024
        ),
    )(
        tokens, w_in_x, w_in_z, w_out, conv_weight, conv_bias[None, :], wxp, w_dt,
        dt_bias[None, :], a_rate.T, d_skip[None, :], segment_ids.reshape(NZ, T),
    )


def solution(mesh):
    placed = (
        P("fsdp", "expert"),
        P(),
        P("fsdp", "expert"),
        P("fsdp", "expert"),
        P(None, "expert"),
        P("expert"),
        P("expert", None),
        P(None, "expert"),
        P("expert"),
        P("expert", None),
        P("expert"),
        P("expert", "fsdp"),
    )
    return jax.shard_map(
        local, mesh=mesh, in_specs=placed, out_specs=P("fsdp", "expert"), check_vma=False
    )
```

```python
import functools
import math

import jax
import jax.numpy as jnp
from jax import lax
from jax.experimental import pallas as pl
from jax.experimental.pallas import tpu as pltpu
from jax.sharding import PartitionSpec as P

F32 = jnp.float32
BF16 = jnp.bfloat16
FAR = 1e30
LOG2E = 1.0 / math.log(2.0)
MESH = pl.DeviceIdType.MESH


def silu(v):
    return v * jax.nn.sigmoid(v)


def dot(a, b):
    return jnp.dot(a, b, preferred_element_type=F32)


def kernel(
    sizes,
    tok, wx, wz, wo, conv_w, conv_b, wxp, wdt, dt_bias, rates, d_skip, ids,
    out,
    TOK, WX, WZ, WO, WP, AX, AZ, XP, HALO, XA, PB, RB, GB, PR,
    DD, DX, SC, Y, HE, PE, KM, KR, KS, SR, MASK, PERM, G, GP, MO, OS, RO,
    local_sem, pair_s, pair_r, tok_s, tok_r, fwd_s, fwd_r, ring_s, ring_r,
    halo_s, halo_r, sum_s, sum_r, all_s, all_r,
    state_s, state_r, reach_s, reach_r, gate_s, gate_r, rest_s, rest_r, out_s, out_r,
):
    NE, NZ, TL, KR_, CH, OC, R, N = sizes
    T, J, H = 2 * TL, TL // 4, NZ // 2
    L = (R + 128) // 128
    CR = PB.shape[1]
    near = min(H, 4)
    far = [near * i for i in range(1, H // near)]
    e = lax.axis_index("expert")
    f = lax.axis_index("fsdp")
    z = lax.div(f, 2)
    c = lax.rem(f, 2)
    o = 1 - c

    def zmod(v):
        return lax.rem(v + 2 * NZ, NZ)

    def emod(v):
        return lax.rem(v + 2 * NE, NE)

    def at(e_, z_, c_):
        return (e_, 2 * z_ + c_)

    def remote(src, dst, ss, rs, dev):
        return pltpu.make_async_remote_copy(
            src_ref=src, dst_ref=dst, send_sem=ss, recv_sem=rs, device_id=dev, device_id_type=MESH
        )

    def span(i, n):
        return pl.ds(pl.multiple_of(i * n, n), n)

    def each(lo, hi, fn):
        def body(k, _):
            fn(k)
            return 0

        lax.fori_loop(lo, hi, body, 0)

    partner = at(e, z, o)

    own = [
        pltpu.make_async_copy(wx.at[:, span(c, CH)], WX.at[z, span(c, KR_)], local_sem.at[0]),
        pltpu.make_async_copy(wz.at[:, span(c, CH)], WZ.at[z, span(c, KR_)], local_sem.at[1]),
        pltpu.make_async_copy(wo.at[span(c, CH)], WO.at[z, :, span(c, OC)], local_sem.at[2]),
        pltpu.make_async_copy(tok, TOK.at[e, span(c, TL)], local_sem.at[3]),
    ]
    for copy in own:
        copy.start()

    row = lax.broadcasted_iota(jnp.int32, (T, T), 0)
    col = lax.broadcasted_iota(jnp.int32, (T, T), 1)
    PERM[...] = (col == lax.rem(row, 8) * J + lax.div(row, 8)).astype(F32).astype(BF16)

    here = jnp.broadcast_to(ids[pl.ds(z, 1), :], (8, T))
    previous = jnp.broadcast_to(ids[pl.ds(zmod(z - 1), 1), :], (8, T))
    lane = lax.broadcasted_iota(jnp.int32, (8, T), 1)
    line = lax.broadcasted_iota(jnp.int32, (8, T), 0)
    same = jnp.zeros((8, T), F32)
    for k in range(1, 4):
        shifted = jnp.where(lane >= k, pltpu.roll(here, k, 1), pltpu.roll(previous, k, 1))
        inside = lane + z * T >= k
        same = jnp.where((line == k - 1) & inside & (shifted == here), 1.0, same)
    MASK[...] = lax.dot_general(
        PERM[...], same.astype(BF16), (((1,), (1,)), ((), ())), preferred_element_type=F32
    )

    barrier = pltpu.get_barrier_semaphore()

    def greet(dev):
        pl.semaphore_signal(barrier, inc=1, device_id=dev, device_id_type=MESH)

    friends = [partner]
    for d in sorted(set(range(1, near + 1)) | set(far)):
        friends += [at(e, zmod(z + d), c), at(e, zmod(z - d), c)]
    count = 1 + 2 * len(set(range(1, near + 1)) | set(far))
    if near == H and NZ == 2 * H and H < 3:
        friends = friends[:-1]
        count -= 1
    for dev in friends:
        greet(dev)

    def greet_plane(k):
        greet(at(emod(e + k), z, c))
        greet(at(emod(e + k), z, o))

    each(1, NE, greet_plane)
    pl.semaphore_wait(barrier, count + 2 * (NE - 1))

    def pair(p, side):
        src = [wx.at[:, span(o, CH)], wz.at[:, span(o, CH)], wo.at[span(o, CH)]][p]
        dst = [WX.at[z, span(side, KR_)], WZ.at[z, span(side, KR_)], WO.at[z, :, span(side, OC)]][p]
        return remote(src, dst, pair_s.at[p], pair_r.at[p], partner)

    pair(0, c).start()

    stacks = [WX, WZ, WO]

    def piece(p, block, h):
        rows = stacks[p].shape[1] // 2
        return stacks[p].at[block, span(h, rows)]

    def hop(p, d, s, h):
        sign = 1 - 2 * d
        block = zmod(z - sign * (s - 1))
        return remote(
            piece(p, block, h), piece(p, block, h),
            ring_s.at[p, d, s, h], ring_r.at[p, d, s, h], at(e, zmod(z + sign), c),
        )

    def arrive(p, d, s, h):
        sign = 1 - 2 * d
        block = zmod(z - sign * s)
        remote(
            piece(p, block, h), piece(p, block, h),
            ring_s.at[p, d, s, h], ring_r.at[p, d, s, h], at(e, zmod(z + sign), c),
        ).wait_recv()

    own[0].wait()
    hop(0, 0, 1, c).start()
    hop(0, 1, 1, c).start()
    pair(1, c).start()
    pair(2, c).start()

    def tok_send(k):
        return remote(
            tok, TOK.at[e, span(c, TL)], tok_s.at[k], tok_r.at[k], at(emod(e + k), z, c)
        )

    def tok_in(k):
        return remote(
            tok, TOK.at[emod(e - k), span(c, TL)], tok_s.at[k], tok_r.at[k], partner
        )

    def tok_fwd(k):
        b = emod(e - k)
        return remote(
            TOK.at[b, span(c, TL)], TOK.at[b, span(c, TL)], fwd_s.at[k], fwd_r.at[k], partner
        )

    def tok_fwd_in(k):
        b = emod(e - k)
        return remote(
            TOK.at[b, span(o, TL)], TOK.at[b, span(o, TL)], fwd_s.at[k], fwd_r.at[k], partner
        )

    pair(0, o).wait_recv()
    hop(0, 0, 1, o).start()
    hop(0, 1, 1, o).start()
    each(1, NE, lambda k: tok_send(k).start())
    own[3].wait()
    tok_fwd(0).start()

    def begin(p):
        own[p].wait()
        pair(p, o).wait_recv()
        for h in (0, 1):
            for d in (0, 1):
                hop(p, d, 1, h).start()

    def rest(d, s):
        block = zmod(z - (1 - 2 * d) * s)
        return remote(WO.at[block], WP.at[block], rest_s.at[d, s], rest_r.at[d, s], partner)

    rests = [(0, s) for s in range(H + 1)] + [(1, s) for s in range(1, H)]

    def step(p, s):
        for h in (0, 1):
            for d in (0, 1):
                if s < H or d == h:
                    arrive(p, d, s, h)
                    if s < H - 1 or (s == H - 1 and d == h):
                        hop(p, d, s + 1, h).start()
        if p == 2:
            for d in range(2 if s < H else 1):
                rest(d, s).start()

    def add(acc, w, block, first=False):
        product = dot(TOK[block], w[block])
        acc[...] = product if first else acc[...] + product

    def add_step(acc, w, s):
        add(acc, w, zmod(z - s))
        if s < H:
            add(acc, w, zmod(z + s))

    def relay(k):
        tok_in(k).wait_recv()
        tok_fwd(k).start()

    relay_at, tokens_at = min(4, H - 1), min(7, H)
    z_after = {2 * i: i for i in range(1, H) if 2 * i < H}
    z_done = len(z_after)
    done = 0
    for s in range(1, H + 1):
        step(0, s)
        if s == 1:
            begin(1)
        if s in z_after:
            step(1, z_after[s])
        if s == H - 1:
            begin(2)
            rest(0, 0).start()
        if s == relay_at:
            each(1, NE, relay)
        if s == tokens_at:
            each(0, NE, lambda k: tok_fwd_in(k).wait_recv())
            add(AX, WX, z, first=True)
        if s >= tokens_at:
            for s_ in range(done + 1, s):
                add_step(AX, WX, s_)
            done = s - 1
    add_step(AX, WX, H)

    position = [0]

    def pump(upto):
        while position[0] < min(upto, H):
            position[0] += 1
            s = position[0]
            if s + z_done <= H:
                step(1, s + z_done)
            step(2, s)
            if s == 1:
                add(AZ, WZ, z, first=True)
                for i in range(1, z_done + 1):
                    add_step(AZ, WZ, i)
            if s + z_done <= H:
                add_step(AZ, WZ, s + z_done)

    perm = PERM[...]
    XP[...] = dot(perm, AX[...].astype(BF16))
    rim = XP.at[pl.ds((J - 3) * 8, 24)]
    halo = remote(rim, HALO, halo_s, halo_r, at(e, zmod(z + 1), c))
    halo.start()
    pump(1)
    halo.wait_recv()
    lane_c = span(c, CH)
    top = lax.broadcasted_iota(jnp.int32, (8, CH), 0) == 0
    early = []
    for i in range(3):
        mine = pltpu.roll(XP[(J - 3 + i) * 8 : (J - 2 + i) * 8], 1, 0)
        theirs = pltpu.roll(HALO[i * 8 : (i + 1) * 8], 1, 0)
        early.append(jnp.where(top, theirs, mine))
    ext = jnp.concatenate(early + [XP[...]], 0)
    conv = conv_b[:, lane_c] + conv_w[3:4, lane_c] * ext[24:]
    for k in range(1, 4):
        conv += conv_w[3 - k : 4 - k, lane_c] * ext[24 - 8 * k : 24 - 8 * k + T] * MASK[:, k - 1 : k]
    x_act = silu(conv).astype(BF16)
    XA[...] = x_act.astype(F32)
    PR[...] = dot(x_act, wxp[span(c, CH), :])

    pump(1)
    blank = [jnp.zeros((CR - 8 * L, 128), F32)] if CR > 8 * L else []

    def pack(q):
        rows = slice(8 * q, 8 * q + 8)
        tiles = [PR[rows, l * 128 : (l + 1) * 128] for l in range(L)]
        PB[q] = jnp.concatenate(tiles + blank, 0).astype(BF16)

    for q in range(2 * NE):
        pack(q)

    def plane(k, rel):
        core = c if rel == 0 else o
        return emod(e + k), core

    def sum_send(k, rel):
        e_, core = plane(k, rel)
        return remote(
            PB.at[core * NE + e_], RB.at[rel * NE + k],
            sum_s.at[rel, k], sum_r.at[rel, k], at(e_, z, core),
        )

    mine = c * NE + e

    def all_send(k, rel):
        e_, core = plane(k, rel)
        return remote(
            GB.at[mine], GB.at[mine], all_s.at[rel, k], all_r.at[rel, k], at(e_, z, core)
        )

    def all_in(k, rel):
        e_, core = plane(-k, rel)
        theirs = core * NE + e_
        return remote(
            GB.at[theirs], GB.at[theirs], all_s.at[rel, k], all_r.at[rel, k], at(e_, z, core)
        )

    def everyone(fn):
        fn(0, 1)

        def both(k):
            fn(k, 1)
            fn(k, 0)

        each(1, NE, both)

    everyone(lambda k, rel: sum_send(k, rel).start())
    pump(2)
    everyone(lambda k, rel: sum_send(k, rel).wait_recv())
    total = PB[mine].astype(F32)
    for k in range(1, 2 * NE):
        total += RB[k].astype(F32)
    GB[mine] = total.astype(BF16)
    everyone(lambda k, rel: all_send(k, rel).start())
    pump(3)
    everyone(lambda k, rel: all_in(k, rel).wait_recv())

    def unpack(q):
        chunk = GB[q].astype(F32)
        for l in range(L):
            PR[8 * q : 8 * q + 8, l * 128 : (l + 1) * 128] = chunk[8 * l : 8 * l + 8]

    for q in range(2 * NE):
        unpack(q)
    pump(4)
    delta = dot(PR[:, :R].astype(BF16), wdt[:, lane_c]) + dt_bias[:, lane_c]
    delta = jnp.maximum(delta, 0.0) + jnp.log1p(jnp.exp(-jnp.abs(delta)))
    DX[...] = delta * XA[...]
    DD[...] = delta + (1.0 - MASK[:, 0:1]) * FAR

    def reach_send(i):
        return remote(KS, SR.at[i], reach_s.at[i], reach_r.at[i], at(e, zmod(z + i + 1), c))

    reach_sum = jnp.zeros((8, CH), F32)
    for j in range(J):
        reach_sum += DD[8 * j : 8 * j + 8, :]
    KS[...] = jnp.broadcast_to(jnp.sum(reach_sum, axis=0, keepdims=True), (N, CH)).astype(BF16)
    for i in range(near):
        reach_send(i).start()

    slope = [rates[n : n + 1, lane_c] * (-LOG2E) for n in range(N)]

    def forward(j, carry):
        hs, reach = carry
        r = pl.ds(pl.multiple_of(j * 8, 8), 8)
        dd, dx, bc = DD[r, :], DX[r, :], PR[r, R : R + 128]
        reach = reach + dd
        SC[r, :] = reach
        y = jnp.zeros((8, CH), F32)
        later = []
        for n in range(N):
            h = jnp.exp2(dd * slope[n]) * hs[n] + dx * bc[:, n : n + 1]
            y = y + h * bc[:, N + n : N + n + 1]
            later.append(h)
        Y[r, :] = y
        return later, reach

    zero = jnp.zeros((8, CH), F32)
    ends, reach = lax.fori_loop(0, J, forward, ([zero] * N, zero), unroll=2)
    sub = lax.broadcasted_iota(jnp.int32, (8, CH), 0)
    states = []
    for n in range(N):
        h, p = ends[n], jnp.exp2(reach * slope[n])
        for d in (1, 2, 4):
            before = sub >= d
            h = h + p * jnp.where(before, pltpu.roll(h, d, 0), 0.0)
            p = p * jnp.where(before, pltpu.roll(p, d, 0), 1.0)
        HE[n] = jnp.where(top, 0.0, pltpu.roll(h, 1, 0))
        PE[n] = jnp.where(top, 1.0, pltpu.roll(p, 1, 0))
        states.append(h[7:8])
    KM[0] = jnp.concatenate(states, 0).astype(BF16)

    steep = rates[:, lane_c] * (-LOG2E)

    def state_send(i):
        d = i + 1 if i < near else far[i - near]
        return remote(
            KM.at[0 if i < near else 1], KR.at[i], state_s.at[i], state_r.at[i],
            at(e, zmod(z + d), c),
        )

    for i in range(near):
        state_send(i).start()
    pump(5)
    distance = jnp.zeros((N, CH), F32)
    for i in range(near):
        reach_send(i).wait_recv()
        state_send(i).wait_recv()
    entering = KR[near - 1].astype(F32)
    for i in range(near - 2, -1, -1):
        entering = jnp.exp2(SR[i].astype(F32) * steep) * entering + KR[i].astype(F32)
    for i in range(near):
        distance += SR[i].astype(F32)
    if far:
        KM[1] = entering.astype(BF16)
        state_send(near).start()
        pump(6)
        state_send(near).wait_recv()
        entering = jnp.exp2(distance * steep) * KR[near].astype(F32) + entering
    pump(7)
    for n in range(N):
        HE[n] = HE[n] + PE[n] * entering[n : n + 1, :]

    def correct(j, _):
        r = pl.ds(pl.multiple_of(j * 8, 8), 8)
        reach, bc = SC[r, :], PR[r, R : R + 128]
        y = Y[r, :]
        for n in range(N):
            y = y + jnp.exp2(reach * slope[n]) * HE[n] * bc[:, N + n : N + n + 1]
        Y[r, :] = y + d_skip[:, lane_c] * XA[r, :]
        return 0

    lax.fori_loop(0, J, correct, 0, unroll=2)
    back = (col == lax.rem(row, J) * 8 + lax.div(row, J)).astype(F32).astype(BF16)
    pump(H)
    gate = silu(dot(perm, AZ[...].astype(BF16)))
    G[...] = dot(back, (Y[...] * gate).astype(BF16)).astype(BF16)

    gated = remote(G.at[span(o, TL)], GP, gate_s, gate_r, partner)
    gated.start()

    def out_send(k):
        return remote(OS.at[k], RO.at[k], out_s.at[k], out_r.at[k], at(emod(e + k), z, c))

    def block_at(k):
        return zmod(e + k)

    def multiply(k):
        MO[k] = dot(G[span(c, TL), :], WO[block_at(k)])

    each(0, NE, multiply)
    for d, s in rests:
        rest(d, s).wait_recv()
    gated.wait_recv()

    def finish(k):
        OS[k] = (MO[k] + dot(GP[...], WP[block_at(k)])).astype(BF16)

    def finish_send(k):
        finish(k)
        out_send(k).start()

    each(1, NE, finish_send)
    finish(0)
    result = OS[0].astype(F32)
    for k in range(1, NE):
        out_send(k).wait_recv()
        result += RO[k].astype(F32)
    out[...] = result.astype(BF16)

    for p in range(3):
        pair(p, c).wait_send()
    halo.wait_send()
    for i in range(near + len(far)):
        state_send(i).wait_send()
    for i in range(near):
        reach_send(i).wait_send()

    def drain(k):
        tok_send(k).wait_send()
        out_send(k).wait_send()

    each(1, NE, drain)

    def drain_all(k, rel):
        sum_send(k, rel).wait_send()
        all_send(k, rel).wait_send()

    everyone(drain_all)

    each(0, NE, lambda k: tok_fwd(k).wait_send())
    gated.wait_send()
    for d, s in rests:
        rest(d, s).wait_send()

    def drain_ring(s):
        for p in range(3):
            for d in range(2):
                for h in range(2):
                    hop(p, d, s, h).wait_send()

    each(1, H, drain_ring)
    for p in range(3):
        for h in range(2):
            hop(p, h, H, h).wait_send()


def local(
    tokens, segment_ids, w_in_x, w_in_z, conv_weight, conv_bias, w_xproj, w_dt, dt_bias,
    a_rate, d_skip, w_out,
):
    NE, NZ = lax.axis_size("expert"), lax.axis_size("fsdp") // 2
    TL, DC = tokens.shape
    KR_, C2 = w_in_x.shape
    CH, OC, R, N = C2 // 2, w_out.shape[1], w_dt.shape[0], a_rate.shape[1]
    T, J, H = 2 * TL, TL // 4, NZ // 2
    PW = R + 128
    wxp = jnp.pad(w_xproj, ((0, 0), (0, PW - w_xproj.shape[1])))
    near = min(H, 4)
    rounds = near + H // near - 1
    CR = -(-PW // 256) * 16
    sizes = (NE, NZ, TL, KR_, CH, OC, R, N)
    V = pltpu.VMEM
    dma = pltpu.SemaphoreType.DMA
    any_space = pl.BlockSpec(memory_space=pl.ANY)
    vmem = pl.BlockSpec(memory_space=pltpu.VMEM)
    return pl.pallas_call(
        functools.partial(kernel, sizes),
        out_shape=jax.ShapeDtypeStruct((TL, DC), BF16),
        in_specs=[any_space] * 4 + [vmem] * 8,
        out_specs=vmem,
        scratch_shapes=[
            V((NE, T, DC), BF16),
            V((NZ, 2 * KR_, CH), BF16),
            V((NZ, 2 * KR_, CH), BF16),
            V((NZ, CH, 2 * OC), BF16),
            V((NZ, CH, 2 * OC), BF16),
            V((T, CH), F32),
            V((T, CH), F32),
            V((T, CH), F32),
            V((24, CH), F32),
            V((T, CH), F32),
            V((2 * NE, CR, 128), BF16),
            V((2 * NE, CR, 128), BF16),
            V((2 * NE, CR, 128), BF16),
            V((T, PW), F32),
            V((T, CH), F32),
            V((T, CH), F32),
            V((T, CH), F32),
            V((T, CH), F32),
            V((N, 8, CH), F32),
            V((N, 8, CH), F32),
            V((2, N, CH), BF16),
            V((rounds, N, CH), BF16),
            V((N, CH), BF16),
            V((near, N, CH), BF16),
            V((T, 8), F32),
            V((T, T), BF16),
            V((T, CH), BF16),
            V((TL, CH), BF16),
            V((NE, TL, DC), F32),
            V((NE, TL, DC), BF16),
            V((NE, TL, DC), BF16),
            dma((4,)),
            dma((3,)), dma((3,)),
            dma((NE,)), dma((NE,)),
            dma((NE,)), dma((NE,)),
            dma((3, 2, H + 1, 2)), dma((3, 2, H + 1, 2)),
            dma(()), dma(()),
            dma((2, NE)), dma((2, NE)),
            dma((2, NE)), dma((2, NE)),
            dma((rounds,)), dma((rounds,)),
            dma((near,)), dma((near,)),
            dma(()), dma(()),
            dma((2, H + 1)), dma((2, H + 1)),
            dma((NE,)), dma((NE,)),
        ],
        compiler_params=pltpu.CompilerParams(
            collective_id=0, has_side_effects=True, vmem_limit_bytes=48 * 1024 * 1024
        ),
    )(
        tokens, w_in_x, w_in_z, w_out, conv_weight, conv_bias[None, :], wxp, w_dt,
        dt_bias[None, :], a_rate.T, d_skip[None, :], segment_ids.reshape(NZ, T),
    )


def solution(mesh):
    placed = (
        P("fsdp", "expert"),
        P(),
        P("fsdp", "expert"),
        P("fsdp", "expert"),
        P(None, "expert"),
        P("expert"),
        P("expert", None),
        P(None, "expert"),
        P("expert"),
        P("expert", None),
        P("expert"),
        P("expert", "fsdp"),
    )
    return jax.shard_map(
        local, mesh=mesh, in_specs=placed, out_specs=P("fsdp", "expert"), check_vma=False
    )
```

```python
import functools
import math

import jax
import jax.numpy as jnp
from jax import lax
from jax.experimental import pallas as pl
from jax.experimental.pallas import tpu as pltpu
from jax.sharding import PartitionSpec as P

F32 = jnp.float32
BF16 = jnp.bfloat16
FAR = 1e30
LOG2E = 1.0 / math.log(2.0)
MESH = pl.DeviceIdType.MESH


def silu(v):
    return v * jax.nn.sigmoid(v)


def dot(a, b):
    return jnp.dot(a, b, preferred_element_type=F32)


def kernel(
    sizes,
    tok, wx, wz, wo, conv_w, conv_b, wxp, wdt, dt_bias, rates, d_skip, ids,
    out,
    TOK, WX, WZ, WO, WP, AX, AZ, XP, HALO, XA, PB, RB, GB, PR,
    DD, DX, SC, Y, HE, PE, KM, KR, KS, SR, MASK, PERM, G, GP, MO, OS, RO,
    local_sem, pair_s, pair_r, tok_s, tok_r, fwd_s, fwd_r, ring_s, ring_r,
    halo_s, halo_r, sum_s, sum_r, all_s, all_r,
    state_s, state_r, reach_s, reach_r, gate_s, gate_r, rest_s, rest_r, out_s, out_r,
):
    NE, NZ, TL, KR_, CH, OC, R, N = sizes
    T, J, H = 2 * TL, TL // 4, NZ // 2
    L = (R + 128) // 128
    CR = PB.shape[1]
    near = min(H, 4)
    far = [near * i for i in range(1, H // near)]
    e = lax.axis_index("expert")
    f = lax.axis_index("fsdp")
    z = lax.div(f, 2)
    c = lax.rem(f, 2)
    o = 1 - c

    def zmod(v):
        return lax.rem(v + 2 * NZ, NZ)

    def emod(v):
        return lax.rem(v + 2 * NE, NE)

    def at(e_, z_, c_):
        return (e_, 2 * z_ + c_)

    def remote(src, dst, ss, rs, dev):
        return pltpu.make_async_remote_copy(
            src_ref=src, dst_ref=dst, send_sem=ss, recv_sem=rs, device_id=dev, device_id_type=MESH
        )

    def span(i, n):
        return pl.ds(pl.multiple_of(i * n, n), n)

    def each(lo, hi, fn):
        def body(k, _):
            fn(k)
            return 0

        lax.fori_loop(lo, hi, body, 0)

    partner = at(e, z, o)

    own = [
        pltpu.make_async_copy(wx.at[:, span(c, CH)], WX.at[z, span(c, KR_)], local_sem.at[0]),
        pltpu.make_async_copy(wz.at[:, span(c, CH)], WZ.at[z, span(c, KR_)], local_sem.at[1]),
        pltpu.make_async_copy(wo.at[span(c, CH)], WO.at[z, :, span(c, OC)], local_sem.at[2]),
        pltpu.make_async_copy(tok, TOK.at[e, span(c, TL)], local_sem.at[3]),
    ]
    for copy in own:
        copy.start()

    row = lax.broadcasted_iota(jnp.int32, (T, T), 0)
    col = lax.broadcasted_iota(jnp.int32, (T, T), 1)
    PERM[...] = (col == lax.rem(row, 8) * J + lax.div(row, 8)).astype(F32).astype(BF16)

    here = jnp.broadcast_to(ids[pl.ds(z, 1), :], (8, T))
    previous = jnp.broadcast_to(ids[pl.ds(zmod(z - 1), 1), :], (8, T))
    lane = lax.broadcasted_iota(jnp.int32, (8, T), 1)
    line = lax.broadcasted_iota(jnp.int32, (8, T), 0)
    same = jnp.zeros((8, T), F32)
    for k in range(1, 4):
        shifted = jnp.where(lane >= k, pltpu.roll(here, k, 1), pltpu.roll(previous, k, 1))
        inside = lane + z * T >= k
        same = jnp.where((line == k - 1) & inside & (shifted == here), 1.0, same)
    MASK[...] = lax.dot_general(
        PERM[...], same.astype(BF16), (((1,), (1,)), ((), ())), preferred_element_type=F32
    )

    barrier = pltpu.get_barrier_semaphore()

    def greet(dev):
        pl.semaphore_signal(barrier, inc=1, device_id=dev, device_id_type=MESH)

    friends = [partner]
    for d in sorted(set(range(1, near + 1)) | set(far)):
        friends += [at(e, zmod(z + d), c), at(e, zmod(z - d), c)]
    count = 1 + 2 * len(set(range(1, near + 1)) | set(far))
    if near == H and NZ == 2 * H and H < 3:
        friends = friends[:-1]
        count -= 1
    for dev in friends:
        greet(dev)

    def greet_plane(k):
        greet(at(emod(e + k), z, c))
        greet(at(emod(e + k), z, o))

    each(1, NE, greet_plane)
    pl.semaphore_wait(barrier, count + 2 * (NE - 1))

    def pair(p, side):
        src = [wx.at[:, span(o, CH)], wz.at[:, span(o, CH)], wo.at[span(o, CH)]][p]
        dst = [WX.at[z, span(side, KR_)], WZ.at[z, span(side, KR_)], WO.at[z, :, span(side, OC)]][p]
        return remote(src, dst, pair_s.at[p], pair_r.at[p], partner)

    pair(0, c).start()

    stacks = [WX, WZ, WO]

    def piece(p, block, h):
        rows = stacks[p].shape[1] // 2
        return stacks[p].at[block, span(h, rows)]

    def hop(p, d, s, h):
        sign = 1 - 2 * d
        block = zmod(z - sign * (s - 1))
        return remote(
            piece(p, block, h), piece(p, block, h),
            ring_s.at[p, d, s, h], ring_r.at[p, d, s, h], at(e, zmod(z + sign), c),
        )

    def arrive(p, d, s, h):
        sign = 1 - 2 * d
        block = zmod(z - sign * s)
        remote(
            piece(p, block, h), piece(p, block, h),
            ring_s.at[p, d, s, h], ring_r.at[p, d, s, h], at(e, zmod(z + sign), c),
        ).wait_recv()

    own[0].wait()
    hop(0, 0, 1, c).start()
    hop(0, 1, 1, c).start()
    pair(1, c).start()
    pair(2, c).start()

    def tok_send(k):
        return remote(
            tok, TOK.at[e, span(c, TL)], tok_s.at[k], tok_r.at[k], at(emod(e + k), z, c)
        )

    def tok_in(k):
        return remote(
            tok, TOK.at[emod(e - k), span(c, TL)], tok_s.at[k], tok_r.at[k], partner
        )

    def tok_fwd(k):
        b = emod(e - k)
        return remote(
            TOK.at[b, span(c, TL)], TOK.at[b, span(c, TL)], fwd_s.at[k], fwd_r.at[k], partner
        )

    def tok_fwd_in(k):
        b = emod(e - k)
        return remote(
            TOK.at[b, span(o, TL)], TOK.at[b, span(o, TL)], fwd_s.at[k], fwd_r.at[k], partner
        )

    pair(0, o).wait_recv()
    hop(0, 0, 1, o).start()
    hop(0, 1, 1, o).start()
    each(1, NE, lambda k: tok_send(k).start())
    own[3].wait()
    tok_fwd(0).start()

    def begin(p):
        own[p].wait()
        pair(p, o).wait_recv()
        for h in (0, 1):
            for d in (0, 1):
                hop(p, d, 1, h).start()

    def rest(d, s):
        block = zmod(z - (1 - 2 * d) * s)
        return remote(WO.at[block], WP.at[block], rest_s.at[d, s], rest_r.at[d, s], partner)

    rests = [(0, s) for s in range(H + 1)] + [(1, s) for s in range(1, H)]

    def step(p, s):
        for h in (0, 1):
            for d in (0, 1):
                if s < H or d == h:
                    arrive(p, d, s, h)
                    if s < H - 1 or (s == H - 1 and d == h):
                        hop(p, d, s + 1, h).start()
        if p == 2:
            for d in range(2 if s < H else 1):
                rest(d, s).start()

    def add(acc, w, block, first=False):
        product = dot(TOK[block], w[block])
        acc[...] = product if first else acc[...] + product

    def add_step(acc, w, s):
        add(acc, w, zmod(z - s))
        if s < H:
            add(acc, w, zmod(z + s))

    def relay(k):
        tok_in(k).wait_recv()
        tok_fwd(k).start()

    relay_at, tokens_at = min(4, H - 1), min(7, H)
    z_after = {2 * i: i for i in range(1, H) if 2 * i < H}
    z_done = len(z_after)
    done = 0
    for s in range(1, H + 1):
        step(0, s)
        if s == 1:
            begin(1)
        if s in z_after:
            step(1, z_after[s])
        if s == H - 1:
            begin(2)
            rest(0, 0).start()
        if s == relay_at:
            each(1, NE, relay)
        if s == tokens_at:
            each(0, NE, lambda k: tok_fwd_in(k).wait_recv())
            add(AX, WX, z, first=True)
        if s >= tokens_at:
            for s_ in range(done + 1, s):
                add_step(AX, WX, s_)
            done = s - 1
    add_step(AX, WX, H)

    position = [0]

    def pump(upto):
        while position[0] < min(upto, H):
            position[0] += 1
            s = position[0]
            if s + z_done <= H:
                step(1, s + z_done)
            step(2, s)
            if s == 1:
                add(AZ, WZ, z, first=True)
                for i in range(1, z_done + 1):
                    add_step(AZ, WZ, i)
            if s + z_done <= H:
                add_step(AZ, WZ, s + z_done)

    perm = PERM[...]
    XP[...] = dot(perm, AX[...].astype(BF16))
    rim = XP.at[pl.ds((J - 3) * 8, 24)]
    halo = remote(rim, HALO, halo_s, halo_r, at(e, zmod(z + 1), c))
    halo.start()
    pump(1)
    halo.wait_recv()
    lane_c = span(c, CH)
    top = lax.broadcasted_iota(jnp.int32, (8, CH), 0) == 0
    early = []
    for i in range(3):
        mine = pltpu.roll(XP[(J - 3 + i) * 8 : (J - 2 + i) * 8], 1, 0)
        theirs = pltpu.roll(HALO[i * 8 : (i + 1) * 8], 1, 0)
        early.append(jnp.where(top, theirs, mine))
    ext = jnp.concatenate(early + [XP[...]], 0)
    conv = conv_b[:, lane_c] + conv_w[3:4, lane_c] * ext[24:]
    for k in range(1, 4):
        conv += conv_w[3 - k : 4 - k, lane_c] * ext[24 - 8 * k : 24 - 8 * k + T] * MASK[:, k - 1 : k]
    x_act = silu(conv).astype(BF16)
    XA[...] = x_act.astype(F32)
    PR[...] = dot(x_act, wxp[span(c, CH), :])

    pump(1)
    blank = [jnp.zeros((CR - 8 * L, 128), F32)] if CR > 8 * L else []

    def pack(q):
        rows = slice(8 * q, 8 * q + 8)
        tiles = [PR[rows, l * 128 : (l + 1) * 128] for l in range(L)]
        PB[q] = jnp.concatenate(tiles + blank, 0).astype(BF16)

    for q in range(2 * NE):
        pack(q)

    def plane(k, rel):
        core = c if rel == 0 else o
        return emod(e + k), core

    def sum_send(k, rel):
        e_, core = plane(k, rel)
        return remote(
            PB.at[core * NE + e_], RB.at[rel * NE + k],
            sum_s.at[rel, k], sum_r.at[rel, k], at(e_, z, core),
        )

    mine = c * NE + e

    def all_send(k, rel):
        e_, core = plane(k, rel)
        return remote(
            GB.at[mine], GB.at[mine], all_s.at[rel, k], all_r.at[rel, k], at(e_, z, core)
        )

    def all_in(k, rel):
        e_, core = plane(-k, rel)
        theirs = core * NE + e_
        return remote(
            GB.at[theirs], GB.at[theirs], all_s.at[rel, k], all_r.at[rel, k], at(e_, z, core)
        )

    def everyone(fn):
        fn(0, 1)

        def both(k):
            fn(k, 1)
            fn(k, 0)

        each(1, NE, both)

    everyone(lambda k, rel: sum_send(k, rel).start())
    pump(3)
    everyone(lambda k, rel: sum_send(k, rel).wait_recv())
    total = PB[mine].astype(F32)
    for k in range(1, 2 * NE):
        total += RB[k].astype(F32)
    GB[mine] = total.astype(BF16)
    everyone(lambda k, rel: all_send(k, rel).start())
    pump(4)
    everyone(lambda k, rel: all_in(k, rel).wait_recv())

    def unpack(q):
        chunk = GB[q].astype(F32)
        for l in range(L):
            PR[8 * q : 8 * q + 8, l * 128 : (l + 1) * 128] = chunk[8 * l : 8 * l + 8]

    for q in range(2 * NE):
        unpack(q)
    pump(4)
    delta = dot(PR[:, :R].astype(BF16), wdt[:, lane_c]) + dt_bias[:, lane_c]
    delta = jnp.maximum(delta, 0.0) + jnp.log1p(jnp.exp(-jnp.abs(delta)))
    DX[...] = delta * XA[...]
    DD[...] = delta + (1.0 - MASK[:, 0:1]) * FAR

    def reach_send(i):
        return remote(KS, SR.at[i], reach_s.at[i], reach_r.at[i], at(e, zmod(z + i + 1), c))

    reach_sum = jnp.zeros((8, CH), F32)
    for j in range(J):
        reach_sum += DD[8 * j : 8 * j + 8, :]
    KS[...] = jnp.broadcast_to(jnp.sum(reach_sum, axis=0, keepdims=True), (N, CH)).astype(BF16)
    for i in range(near):
        reach_send(i).start()

    slope = [rates[n : n + 1, lane_c] * (-LOG2E) for n in range(N)]

    def forward(j, carry):
        hs, reach = carry
        r = pl.ds(pl.multiple_of(j * 8, 8), 8)
        dd, dx, bc = DD[r, :], DX[r, :], PR[r, R : R + 128]
        reach = reach + dd
        SC[r, :] = reach
        y = jnp.zeros((8, CH), F32)
        later = []
        for n in range(N):
            h = jnp.exp2(dd * slope[n]) * hs[n] + dx * bc[:, n : n + 1]
            y = y + h * bc[:, N + n : N + n + 1]
            later.append(h)
        Y[r, :] = y
        return later, reach

    zero = jnp.zeros((8, CH), F32)
    ends, reach = lax.fori_loop(0, J, forward, ([zero] * N, zero), unroll=4)
    sub = lax.broadcasted_iota(jnp.int32, (8, CH), 0)
    states = []
    for n in range(N):
        h, p = ends[n], jnp.exp2(reach * slope[n])
        for d in (1, 2, 4):
            before = sub >= d
            h = h + p * jnp.where(before, pltpu.roll(h, d, 0), 0.0)
            p = p * jnp.where(before, pltpu.roll(p, d, 0), 1.0)
        HE[n] = jnp.where(top, 0.0, pltpu.roll(h, 1, 0))
        PE[n] = jnp.where(top, 1.0, pltpu.roll(p, 1, 0))
        states.append(h[7:8])
    KM[0] = jnp.concatenate(states, 0).astype(BF16)

    steep = rates[:, lane_c] * (-LOG2E)

    def state_send(i):
        d = i + 1 if i < near else far[i - near]
        return remote(
            KM.at[0 if i < near else 1], KR.at[i], state_s.at[i], state_r.at[i],
            at(e, zmod(z + d), c),
        )

    for i in range(near):
        state_send(i).start()
    pump(5)
    distance = jnp.zeros((N, CH), F32)
    for i in range(near):
        reach_send(i).wait_recv()
        state_send(i).wait_recv()
    entering = KR[near - 1].astype(F32)
    for i in range(near - 2, -1, -1):
        entering = jnp.exp2(SR[i].astype(F32) * steep) * entering + KR[i].astype(F32)
    for i in range(near):
        distance += SR[i].astype(F32)
    if far:
        KM[1] = entering.astype(BF16)
        state_send(near).start()
        pump(6)
        state_send(near).wait_recv()
        entering = jnp.exp2(distance * steep) * KR[near].astype(F32) + entering
    pump(7)
    for n in range(N):
        HE[n] = HE[n] + PE[n] * entering[n : n + 1, :]

    def correct(j, _):
        r = pl.ds(pl.multiple_of(j * 8, 8), 8)
        reach, bc = SC[r, :], PR[r, R : R + 128]
        y = Y[r, :]
        for n in range(N):
            y = y + jnp.exp2(reach * slope[n]) * HE[n] * bc[:, N + n : N + n + 1]
        Y[r, :] = y + d_skip[:, lane_c] * XA[r, :]
        return 0

    lax.fori_loop(0, J, correct, 0, unroll=4)
    back = (col == lax.rem(row, J) * 8 + lax.div(row, J)).astype(F32).astype(BF16)
    pump(H)
    gate = silu(dot(perm, AZ[...].astype(BF16)))
    G[...] = dot(back, (Y[...] * gate).astype(BF16)).astype(BF16)

    gated = remote(G.at[span(o, TL)], GP, gate_s, gate_r, partner)
    gated.start()

    def out_send(k):
        return remote(OS.at[k], RO.at[k], out_s.at[k], out_r.at[k], at(emod(e + k), z, c))

    def block_at(k):
        return zmod(e + k)

    def multiply(k):
        MO[k] = dot(G[span(c, TL), :], WO[block_at(k)])

    each(0, NE, multiply)
    for d, s in rests:
        rest(d, s).wait_recv()
    gated.wait_recv()

    def finish(k):
        OS[k] = (MO[k] + dot(GP[...], WP[block_at(k)])).astype(BF16)

    def finish_send(k):
        finish(k)
        out_send(k).start()

    each(1, NE, finish_send)
    finish(0)
    result = OS[0].astype(F32)
    for k in range(1, NE):
        out_send(k).wait_recv()
        result += RO[k].astype(F32)
    out[...] = result.astype(BF16)

    for p in range(3):
        pair(p, c).wait_send()
    halo.wait_send()
    for i in range(near + len(far)):
        state_send(i).wait_send()
    for i in range(near):
        reach_send(i).wait_send()

    def drain(k):
        tok_send(k).wait_send()
        out_send(k).wait_send()

    each(1, NE, drain)

    def drain_all(k, rel):
        sum_send(k, rel).wait_send()
        all_send(k, rel).wait_send()

    everyone(drain_all)

    each(0, NE, lambda k: tok_fwd(k).wait_send())
    gated.wait_send()
    for d, s in rests:
        rest(d, s).wait_send()

    def drain_ring(s):
        for p in range(3):
            for d in range(2):
                for h in range(2):
                    hop(p, d, s, h).wait_send()

    each(1, H, drain_ring)
    for p in range(3):
        for h in range(2):
            hop(p, h, H, h).wait_send()


def local(
    tokens, segment_ids, w_in_x, w_in_z, conv_weight, conv_bias, w_xproj, w_dt, dt_bias,
    a_rate, d_skip, w_out,
):
    NE, NZ = lax.axis_size("expert"), lax.axis_size("fsdp") // 2
    TL, DC = tokens.shape
    KR_, C2 = w_in_x.shape
    CH, OC, R, N = C2 // 2, w_out.shape[1], w_dt.shape[0], a_rate.shape[1]
    T, J, H = 2 * TL, TL // 4, NZ // 2
    PW = R + 128
    wxp = jnp.pad(w_xproj, ((0, 0), (0, PW - w_xproj.shape[1])))
    near = min(H, 4)
    rounds = near + H // near - 1
    CR = -(-PW // 256) * 16
    sizes = (NE, NZ, TL, KR_, CH, OC, R, N)
    V = pltpu.VMEM
    dma = pltpu.SemaphoreType.DMA
    any_space = pl.BlockSpec(memory_space=pl.ANY)
    vmem = pl.BlockSpec(memory_space=pltpu.VMEM)
    return pl.pallas_call(
        functools.partial(kernel, sizes),
        out_shape=jax.ShapeDtypeStruct((TL, DC), BF16),
        in_specs=[any_space] * 4 + [vmem] * 8,
        out_specs=vmem,
        scratch_shapes=[
            V((NE, T, DC), BF16),
            V((NZ, 2 * KR_, CH), BF16),
            V((NZ, 2 * KR_, CH), BF16),
            V((NZ, CH, 2 * OC), BF16),
            V((NZ, CH, 2 * OC), BF16),
            V((T, CH), F32),
            V((T, CH), F32),
            V((T, CH), F32),
            V((24, CH), F32),
            V((T, CH), F32),
            V((2 * NE, CR, 128), BF16),
            V((2 * NE, CR, 128), BF16),
            V((2 * NE, CR, 128), BF16),
            V((T, PW), F32),
            V((T, CH), F32),
            V((T, CH), F32),
            V((T, CH), F32),
            V((T, CH), F32),
            V((N, 8, CH), F32),
            V((N, 8, CH), F32),
            V((2, N, CH), BF16),
            V((rounds, N, CH), BF16),
            V((N, CH), BF16),
            V((near, N, CH), BF16),
            V((T, 8), F32),
            V((T, T), BF16),
            V((T, CH), BF16),
            V((TL, CH), BF16),
            V((NE, TL, DC), F32),
            V((NE, TL, DC), BF16),
            V((NE, TL, DC), BF16),
            dma((4,)),
            dma((3,)), dma((3,)),
            dma((NE,)), dma((NE,)),
            dma((NE,)), dma((NE,)),
            dma((3, 2, H + 1, 2)), dma((3, 2, H + 1, 2)),
            dma(()), dma(()),
            dma((2, NE)), dma((2, NE)),
            dma((2, NE)), dma((2, NE)),
            dma((rounds,)), dma((rounds,)),
            dma((near,)), dma((near,)),
            dma(()), dma(()),
            dma((2, H + 1)), dma((2, H + 1)),
            dma((NE,)), dma((NE,)),
        ],
        compiler_params=pltpu.CompilerParams(
            collective_id=0, has_side_effects=True, vmem_limit_bytes=48 * 1024 * 1024
        ),
    )(
        tokens, w_in_x, w_in_z, w_out, conv_weight, conv_bias[None, :], wxp, w_dt,
        dt_bias[None, :], a_rate.T, d_skip[None, :], segment_ids.reshape(NZ, T),
    )


def solution(mesh):
    placed = (
        P("fsdp", "expert"),
        P(),
        P("fsdp", "expert"),
        P("fsdp", "expert"),
        P(None, "expert"),
        P("expert"),
        P("expert", None),
        P(None, "expert"),
        P("expert"),
        P("expert", None),
        P("expert"),
        P("expert", "fsdp"),
    )
    return jax.shard_map(
        local, mesh=mesh, in_specs=placed, out_specs=P("fsdp", "expert"), check_vma=False
    )
```
